512 devices in a mesh: row: 16 (over x_lo, y, core), col: 32 (over z, x_hi).
Axes of the slice: x: 4 (x_hi: 2, x_lo: 2; x = x_hi * 2 + x_lo), y: 4, z: 16, core: 2. Of those that a mesh axis runs over, the one named last changes fastest.
Arguments:
- pair: bfloat16 [384, 384, 128], P('row', 'col'), may hold values from -6 to 6
- crop: int32 [384], replicated, may hold values from 0 to 3, never falling along the last dimension, each value on 1 to 192 neighbouring positions
- in_gain: float32 [128], replicated, may hold values from 0.25 to 1.75
- in_bias: float32 [128], replicated, may hold values from -2 to 2
- in_weights: bfloat16 [128, 640], replicated, may hold values from -0.5 to 0.5
- out_gain: float32 [128], replicated, may hold values from 0.25 to 1.75
- out_bias: float32 [128], replicated, may hold values from -2 to 2
- out_weights: bfloat16 [128, 128], replicated, may hold values from -0.5 to 0.5
- cotangent: bfloat16 [384, 384, 128], P('row', 'col'), may hold values from -6 to 6
Outputs:
- update: bfloat16 [384, 384, 128], P('row', 'col')
- pair_grad: bfloat16 [384, 384, 128], P('row', 'col')
The draws below stay inside these ranges and needn't reach their ends.
Inputs may be any that keep to these rules, and one draw needn't show every extreme that they name: crop numbers never fall along the row; every crop is 1 to 192 residues long, and one crop is exactly 192 long.
All inputs are finite; a program needn't handle non-finite values.
Results may differ from the reference program's by a relative error of at most 0.0076.
Values may be sent and summed in bfloat16 or wider, within the bound.
No kernel may reach another device: no remote copies, remote signals or barrier semaphores. Data moves between devices by JAX's collectives and lax.ppermute only.
A program may use at most 128 MiB of HBM per device.

```python
import math
import jax
import jax.numpy as jnp
import numpy as np
from jax import lax

C = 128
H = 128
CROPS = 4
N_RES = 384
CROP_MOST = 192


def shard_levels(own_key, shape, shards, smallest, largest):
    def one(axis_at, parts):
        draws = jax.random.uniform(jax.random.fold_in(jax.random.fold_in(own_key, 6), axis_at), (parts,), jnp.float32, smallest / len(shards), largest / len(shards))
        return jnp.repeat(jnp.exp(draws), shape[axis_at] // parts).reshape((-1,) + (1,) * (len(shape) - axis_at - 1))

    factor_of = one(*shards[0])
    for cut in shards[1:]:
        factor_of = factor_of * one(*cut)
    return factor_of


def profile(amount, total, bound, slope):
    portions = [(1 << 20) // math.isqrt(rank ** slope) + 1 for rank in range(2, amount + 1)]
    spare, holding = total - bound - (amount - 1), [1] * (amount - 1)
    while spare > 0:
        free = [i for i in range(amount - 1) if holding[i] < bound]
        pool, budget = sum([portions[i] for i in free]), spare
        for i in free:
            extra = min(bound - holding[i], max(1, budget * portions[i] // pool), spare)
            holding[i] = holding[i] + extra
            spare = spare - extra
    return np.array([bound] + holding)


def uneven(key, number_of, total, reach, lean):
    if number_of == 2:
        one = jax.random.randint(key, (), max(1, total - reach), min(reach, total - 1) + 1)
        return jnp.stack([one, total - one])
    lengths = jnp.asarray(profile(number_of, total, reach, lean), jnp.int32)
    twos = (number_of - 1) // 2
    source_of, taker = lengths[1:1 + 2 * twos:2], lengths[2:2 + 2 * twos:2]
    slack = jnp.minimum(source_of - 1, reach - taker)
    shifted = jax.random.randint(jax.random.fold_in(key, 1), (twos,), 0, 1 << 20) % (slack + 1)
    lengths = lengths.at[1:1 + 2 * twos:2].set(source_of - shifted).at[2:2 + 2 * twos:2].set(taker + shifted)
    return lengths[jax.random.permutation(jax.random.fold_in(key, 2), number_of)]


def centred(own_key, shape, spread, most, shards=(), held_as=jnp.bfloat16):
    result = spread * jax.random.normal(own_key, shape, jnp.float32)
    if shards:
        result = result * shard_levels(own_key, shape, shards, -0.22, 0.18)
    return jnp.clip(result, -most, most).astype(held_as)


def setup_inputs(seed: int = 0) -> dict:
    arg_keys = jax.random.split(jax.random.key(seed), 10)
    return {
        "pair": centred(arg_keys[0], (N_RES, N_RES, C), 1.0, 6.0, ((0, 16), (1, 32))),
        "crop": jnp.searchsorted(jnp.cumsum(uneven(arg_keys[1], CROPS, N_RES, CROP_MOST, 0)), jnp.arange(N_RES), side="right").astype(jnp.int32),
        "in_gain": jnp.clip(1.0 + 0.15 * jax.random.normal(arg_keys[2], (C,), jnp.float32), 0.25, 1.75),
        "in_bias": centred(arg_keys[3], (C,), 0.5, 2.0, (), jnp.float32),
        "in_weights": centred(arg_keys[4], (C, 4 * H + C), C ** -0.5, 0.5),
        "out_gain": jnp.clip(1.0 + 0.15 * jax.random.normal(arg_keys[5], (H,), jnp.float32), 0.25, 1.75),
        "out_bias": centred(arg_keys[6], (H,), 0.5, 2.0, (), jnp.float32),
        "out_weights": centred(arg_keys[7], (H, C), H ** -0.5, 0.5),
        "cotangent": centred(arg_keys[8], (N_RES, N_RES, C), 1.0, 6.0, ((0, 16), (1, 32))),
    }


norm_eps = 1e-05

def normalize(values):
    average = lax.optimization_barrier(jnp.mean(values, axis=-1, keepdims=True))
    centered = values - average
    inv_std = lax.rsqrt(lax.optimization_barrier(jnp.mean(centered * centered, axis=-1, keepdims=True)) + norm_eps)
    return (centered * inv_std, inv_std)

def norm_back(upstream_grad, normalized, inv_std):
    first_mean = lax.optimization_barrier(jnp.mean(upstream_grad, axis=-1, keepdims=True))
    second_mean = lax.optimization_barrier(jnp.mean(upstream_grad * normalized, axis=-1, keepdims=True))
    return inv_std * (upstream_grad - first_mean - normalized * second_mean)

def reference(pair, crop, in_gain, in_bias, in_weights, out_gain, out_bias, out_weights, cotangent):
    residues = pair.shape[0]
    pair_width = pair.shape[2]
    hidden_width = out_weights.shape[0]
    inside = (crop[:, None] == crop[None, :]).astype(jnp.float32)[:, :, None]
    pair_hat, inv_in = normalize(pair.astype(jnp.float32))
    normed = (pair_hat * in_gain + in_bias).astype(jnp.bfloat16)
    flat_normed = normed.reshape(residues * residues, pair_width)

    def project(first_col, last_col):
        block = jnp.dot(flat_normed, in_weights[:, first_col:last_col], preferred_element_type=jnp.float32)
        return block.reshape(residues, residues, last_col - first_col)
    left_val = project(0, hidden_width)
    right_val = project(hidden_width, 2 * hidden_width)
    left_sig = jax.nn.sigmoid(project(2 * hidden_width, 3 * hidden_width))
    right_sig = jax.nn.sigmoid(project(3 * hidden_width, 4 * hidden_width))
    gate = jax.nn.sigmoid(project(4 * hidden_width, 4 * hidden_width + pair_width))
    left_gated = (inside * left_sig * left_val).astype(jnp.bfloat16)
    right_gated = (inside * right_sig * right_val).astype(jnp.bfloat16)
    left_wide = left_gated.astype(jnp.float32)
    right_wide = right_gated.astype(jnp.float32)
    tri = jnp.einsum('kih,kjh->ijh', left_wide, right_wide)
    tri_hat, inv_out = normalize(tri)
    normed_out = (tri_hat * out_gain + out_bias).astype(jnp.bfloat16)
    gated_value = jnp.dot(normed_out.reshape(-1, hidden_width), out_weights, preferred_element_type=jnp.float32).reshape(residues, residues, pair_width)
    update = (gate * gated_value).astype(jnp.bfloat16)
    upstream = cotangent.astype(jnp.float32)
    d_value = (upstream * gate).astype(jnp.bfloat16)
    d_outpre = upstream * gated_value * gate * (1.0 - gate)
    d_normed = jnp.dot(d_value.reshape(-1, pair_width), out_weights.T, preferred_element_type=jnp.float32).reshape(residues, residues, hidden_width)
    d_tri = norm_back(d_normed * out_gain, tri_hat, inv_out).astype(jnp.bfloat16)
    d_tri_wide = d_tri.astype(jnp.float32)
    d_left = jnp.einsum('kjh,ijh->kih', right_wide, d_tri_wide)
    d_right = jnp.einsum('kih,ijh->kjh', left_wide, d_tri_wide)
    d_proj = jnp.concatenate([d_left * inside * left_sig, d_right * inside * right_sig, d_left * inside * left_val * left_sig * (1.0 - left_sig), d_right * inside * right_val * right_sig * (1.0 - right_sig), d_outpre], axis=-1).astype(jnp.bfloat16)
    d_normed_in = jnp.dot(d_proj.reshape(residues * residues, -1), in_weights.T, preferred_element_type=jnp.float32).reshape(residues, residues, pair_width)
    pair_grad = norm_back(d_normed_in * in_gain, pair_hat, inv_in).astype(jnp.bfloat16)
    return (update, pair_grad)
```

```python
import jax
import jax.numpy as jnp
from jax import lax
from jax.experimental import pallas as pl
from jax.experimental.pallas import tpu as pltpu
from jax.sharding import Mesh, PartitionSpec as P

norm_eps = 1e-05
f32 = jnp.float32
bf16 = jnp.bfloat16
ROWS = ("xlo", "y", "core")
COLS = ("zhi", "zlo", "xhi")
OWNERS = ("zlo", "xhi", "xlo", "y", "core")
TK, TI, PAD = 24, 12, 16
LANES = TK * PAD
E, R, Q = 8, 16, 4
C = 128
N = 384
FOLD = N // 2
RF = R // 2


def dot(first_op, second_op, dims):
    return lax.dot_general(first_op, second_op, (dims, ((), ())), preferred_element_type=f32)


def swap_blocks(parts):
    parts = list(parts)
    block = lax.broadcasted_iota(jnp.int32, parts[0].shape, 1) // PAD
    for step in (4, 2, 1):
        upper = (block & step) != 0
        for a in range(8):
            if a & step:
                continue
            b = a | step
            low, high = parts[a], parts[b]
            parts[a] = jnp.where(upper, pltpu.roll(high, step * PAD, 1), low)
            parts[b] = jnp.where(upper, high, pltpu.roll(low, 128 - step * PAD, 1))
    return parts


def as_column(row):
    return jnp.broadcast_to(row, (C, C)).T[:, :1]


def padded_rows(tile, scratch):
    scratch[...] = jnp.zeros_like(scratch)
    scratch[:, :TI, :] = tile.astype(f32)
    return scratch[...].reshape(LANES, C)


def norm_rows(values):
    centered = values - jnp.mean(values, axis=1, keepdims=True)
    inv_std = lax.rsqrt(jnp.mean(centered * centered, axis=1, keepdims=True) + norm_eps)
    return centered * inv_std, inv_std


def put_channels(scratch, values, slot, stride):
    for t in range(3):
        scratch[pl.ds(slot + t, C, stride=stride), :] = values[:, 128 * t : 128 * (t + 1)]
    scratch[pl.ds(slot + 3, C, stride=stride), :] = jnp.zeros((C, 128), f32)


def get_channels(scratch, slot, stride):
    return jnp.concatenate(
        [scratch[pl.ds(slot + t, C, stride=stride), :] for t in range(3)], axis=1
    )


def project_kernel(pair, crop, gain, bias, weights, send, projected, inside, padded, slots):
    row_pos = lax.axis_index(ROWS)
    col_pos = lax.axis_index(COLS)
    lane = lax.broadcasted_iota(jnp.int32, (N, LANES), 1)
    residue = lax.broadcasted_iota(jnp.int32, (N, LANES), 0)
    crops = jnp.broadcast_to(crop[...].astype(f32), (8, N)).astype(bf16)
    pick_row = (residue == row_pos * TK + lane // PAD).astype(f32).astype(bf16)
    pick_col = (residue == col_pos * TI + lane % PAD).astype(f32).astype(bf16)
    crop_rows = dot(crops, pick_row, ((1,), (0,)))
    crop_cols = dot(crops, pick_col, ((1,), (0,)))
    lane8 = lax.broadcasted_iota(jnp.int32, (8, LANES), 1)
    same = (crop_rows == crop_cols) & (lane8 % PAD < TI)
    inside[...] = same.astype(f32)
    mask = same.astype(f32)[:1, :]

    hat, _ = norm_rows(padded_rows(pair[...], padded))
    normed = (hat * gain[...] + bias[...]).astype(bf16)
    proj = dot(weights[...].T, normed, ((1,), (1,)))
    projected[...] = proj
    left = mask * jax.nn.sigmoid(proj[2 * C : 3 * C]) * proj[:C]
    right = mask * jax.nn.sigmoid(proj[3 * C : 4 * C]) * proj[C : 2 * C]
    put_channels(slots, left, 0, 8)
    put_channels(slots, right, 4, 8)
    send[...] = slots[...].astype(bf16)


def collect_kernel(received, left, right, slots):
    slots[...] = received[...].astype(f32)
    parts = [
        jnp.concatenate(
            [
                slots[pl.ds(8 * R * e + 4 * side + t, R, stride=8), :]
                for side in range(2)
                for t in range(3)
            ],
            axis=0,
        )
        for e in range(E)
    ]
    parts = swap_blocks(parts)
    for side, out in enumerate((left, right)):
        pieces = []
        for t in range(3):
            for k in range(8):
                at = (3 * side + t) * R
                pieces.append(parts[k][at : at + RF] + parts[k][at + RF : at + R])
        out[...] = jnp.concatenate(pieces, axis=0).astype(bf16)


def reorder(transposed):
    shape = (N, Q * 128) if transposed else (Q * 128, N)
    wide = lax.broadcasted_iota(jnp.int32, shape, 1 if transposed else 0)
    target = lax.broadcasted_iota(jnp.int32, shape, 0 if transposed else 1)
    e = (wide // PAD) % E
    within = (e % 2) * TI + wide % PAD
    position = (wide // 128) * 4 + e // 2
    hit = (target == within * R + position) & (wide % PAD < TI)
    return hit.astype(f32).astype(bf16)


def triangle_kernel(left_all, right, send, slots):
    tri = jnp.concatenate(
        [dot(left_all[q], right[...], ((0,), (0,))) for q in range(Q)], axis=0
    ).astype(bf16)
    tri = dot(reorder(True), tri, ((1,), (0,)))
    parts = [
        jnp.concatenate([tri[(8 * t + i) * R : (8 * t + i + 1) * R] for t in range(3)], axis=0)
        for i in range(8)
    ]
    parts = swap_blocks(parts)
    for e in range(E):
        for t in range(3):
            slots[pl.ds(4 * R * e + t, R, stride=4), :] = parts[e][t * R : (t + 1) * R]
        slots[pl.ds(4 * R * e + 3, R, stride=4), :] = jnp.zeros((R, 128), f32)
    send[...] = slots[...].astype(bf16)


def output_kernel(
    received, out_pre, inside, cotangent, gain, bias, weights, update, d_outpre, send, padded, slots
):
    mask = inside[:1, :]
    slots[...] = received[...].astype(f32)
    tri = jnp.where(mask > 0, get_channels(slots, 0, 4), 0.0)
    centered = tri - jnp.mean(tri, axis=0, keepdims=True)
    inv_out = lax.rsqrt(jnp.mean(centered * centered, axis=0, keepdims=True) + norm_eps)
    tri_hat = centered * inv_out
    gain_col = as_column(gain[...])
    normed_out = (tri_hat * gain_col + as_column(bias[...])).astype(bf16)
    gated_value = dot(weights[...].T, normed_out, ((1,), (0,)))
    gate = jax.nn.sigmoid(out_pre[...])
    new = (gate * gated_value).T.reshape(TK, PAD, C)
    update[...] = new[:, :TI, :].astype(bf16)
    upstream = padded_rows(cotangent[...], padded).T
    d_value = (upstream * gate).astype(bf16)
    d_outpre[...] = (upstream * gated_value * gate * (1.0 - gate)).astype(bf16)
    grad = dot(weights[...], d_value, ((1,), (0,))) * gain_col
    first_mean = jnp.mean(grad, axis=0, keepdims=True)
    second_mean = jnp.mean(grad * tri_hat, axis=0, keepdims=True)
    d_tri = inv_out * (grad - first_mean - tri_hat * second_mean)
    put_channels(slots, jnp.where(mask > 0, d_tri, 0.0), 0, 4)
    send[...] = slots[...].astype(bf16)


def back_kernel(received, left_all, right, d_right, send, slots):
    slots[...] = received[...].astype(f32)
    parts = [
        jnp.concatenate(
            [slots[pl.ds(4 * R * e + t, R, stride=4), :] for t in range(3)], axis=0
        )
        for e in range(E)
    ]
    parts = swap_blocks(parts)
    d_tri = jnp.concatenate(
        [parts[i][t * R : (t + 1) * R] for t in range(3) for i in range(8)], axis=0
    ).astype(bf16)
    d_tri = dot(reorder(False), d_tri, ((1,), (0,))).astype(bf16)
    total = jnp.zeros((FOLD, 128), f32)
    for q in range(Q):
        block = d_tri[128 * q : 128 * (q + 1)]
        total = total + dot(left_all[q], block, ((1,), (0,)))
        send[q] = dot(right[...], block, ((1,), (1,))).astype(bf16)
    d_right[...] = total


def spread_kernel(received, d_right, send, slots):
    d_left = received[0].astype(f32)
    for q in range(1, Q):
        d_left = d_left + received[q].astype(f32)
    sides = (d_left, d_right[...])
    parts = [
        jnp.concatenate(
            [
                sides[side][(8 * t + k) * RF : (8 * t + k + 1) * RF]
                for side in range(2)
                for t in range(3)
            ],
            axis=0,
        )
        for k in range(8)
    ]
    parts = swap_blocks(parts)
    for e in range(E):
        for side in range(2):
            for t in range(3):
                piece = parts[e][(3 * side + t) * RF : (3 * side + t + 1) * RF]
                for half in range(2):
                    start = 8 * (R * e + RF * half) + 4 * side + t
                    slots[pl.ds(start, RF, stride=8), :] = piece
            slots[pl.ds(8 * R * e + 4 * side + 3, R, stride=8), :] = jnp.zeros((R, 128), f32)
    send[...] = slots[...].astype(bf16)


def input_kernel(
    received, projected, inside, d_outpre, pair, gain, weights, pair_grad, padded, slots
):
    slots[...] = received[...].astype(f32)
    mask = inside[:1, :]
    d_left = get_channels(slots, 0, 8) * mask
    d_right = get_channels(slots, 4, 8) * mask
    left_val, right_val = projected[:C], projected[C : 2 * C]
    left_sig = jax.nn.sigmoid(projected[2 * C : 3 * C])
    right_sig = jax.nn.sigmoid(projected[3 * C : 4 * C])
    d_proj = jnp.concatenate(
        [
            (d_left * left_sig).astype(bf16),
            (d_right * right_sig).astype(bf16),
            (d_left * left_val * left_sig * (1.0 - left_sig)).astype(bf16),
            (d_right * right_val * right_sig * (1.0 - right_sig)).astype(bf16),
            d_outpre[...],
        ],
        axis=0,
    )
    grad = dot(weights[...], d_proj, ((1,), (0,))).T * gain[...]
    hat, inv_in = norm_rows(padded_rows(pair[...], padded))
    first_mean = jnp.mean(grad, axis=1, keepdims=True)
    second_mean = jnp.mean(grad * hat, axis=1, keepdims=True)
    result = (inv_in * (grad - first_mean - hat * second_mean)).reshape(TK, PAD, C)
    pair_grad[...] = result[:, :TI, :].astype(bf16)


def call(kernel, outs, scratch, *operands):
    return pl.pallas_call(
        kernel,
        out_shape=[jax.ShapeDtypeStruct(shape, dtype) for shape, dtype in outs],
        in_specs=[pl.BlockSpec(memory_space=pltpu.VMEM)] * len(operands),
        out_specs=[pl.BlockSpec(memory_space=pltpu.VMEM)] * len(outs),
        scratch_shapes=[pltpu.VMEM(shape, f32) for shape in scratch],
        compiler_params=pltpu.CompilerParams(vmem_limit_bytes=40 * 1024 * 1024),
        name=kernel.__name__,
    )(*operands)


def exchange(values, height):
    moved = lax.all_to_all(values.reshape(C, height, 128), OWNERS, 0, 0, tiled=True)
    return moved.reshape(C * height, 128)


def body(pair, crop, in_gain, in_bias, in_weights, out_gain, out_bias, out_weights, cotangent):
    tile = (TK, PAD, C)
    in_gain, in_bias, out_gain, out_bias = (
        v.reshape(1, C) for v in (in_gain, in_bias, out_gain, out_bias)
    )
    send, projected, inside = call(
        project_kernel,
        [((8 * C, 128), bf16), ((5 * C, LANES), f32), ((8, LANES), f32)],
        [tile, (8 * C, 128)],
        pair, crop.reshape(1, N), in_gain, in_bias, in_weights,
    )
    left, right = call(
        collect_kernel,
        [((FOLD, 128), bf16)] * 2,
        [(8 * C, 128)],
        exchange(send, 8),
    )
    left_all = lax.all_gather(left, "zhi", axis=0)
    (send,) = call(
        triangle_kernel, [((4 * C, 128), bf16)], [(4 * C, 128)], left_all, right
    )
    update, d_outpre, send = call(
        output_kernel,
        [((TK, TI, C), bf16), ((C, LANES), bf16), ((4 * C, 128), bf16)],
        [tile, (4 * C, 128)],
        exchange(send, 4), projected[4 * C :], inside, cotangent, out_gain, out_bias, out_weights,
    )
    d_right, send = call(
        back_kernel,
        [((FOLD, 128), f32), ((Q, FOLD, 128), bf16)],
        [(4 * C, 128)],
        exchange(send, 4), left_all, right,
    )
    partial = lax.all_to_all(send, "zhi", 0, 0, tiled=True)
    (send,) = call(
        spread_kernel, [((8 * C, 128), bf16)], [(8 * C, 128)], partial, d_right
    )
    (pair_grad,) = call(
        input_kernel,
        [((TK, TI, C), bf16)],
        [tile, (8 * C, 128)],
        exchange(send, 8), projected, inside, d_outpre, pair, in_gain, in_weights,
    )
    return update, pair_grad


def solution(mesh):
    split = Mesh(mesh.devices.reshape(2, 4, 2, 4, 4, 2), ROWS + COLS)
    tiles = P(ROWS, COLS, None)
    in_specs = (tiles, P(), P(), P(), P(), P(), P(), P(), tiles)
    return jax.shard_map(
        body, mesh=split, in_specs=in_specs, out_specs=(tiles, tiles), check_vma=False
    )
```

```python
import jax
import jax.numpy as jnp
from jax import lax
from jax.experimental import pallas as pl
from jax.experimental.pallas import tpu as pltpu
from jax.sharding import Mesh, PartitionSpec as P

norm_eps = 1e-05
f32 = jnp.float32
bf16 = jnp.bfloat16
ROWS = ("xlo", "y", "core")
COLS = ("zhi", "zlo", "xhi")
OWNERS = ("zlo", "xhi", "xlo", "y", "core")
TK, TI, PAD = 24, 12, 16
LANES = TK * PAD
E, R, Q = 4, 16, 8
HELD = 8 // E
WIDTH = 128 // HELD
C = 128
N = 384
FOLD = N // 2
PACK = FOLD * TI // PAD
GROUP = FOLD - PACK
RF = R // 2
BOTH = (C // HELD, 2 * HELD, LANES)
ONE = (C // HELD, HELD, LANES)


def dot(first_op, second_op, dims):
    return lax.dot_general(first_op, second_op, (dims, ((), ())), preferred_element_type=f32)


def swap_blocks(parts):
    parts = list(parts)
    block = lax.broadcasted_iota(jnp.int32, parts[0].shape, 1) // PAD
    for step in (4, 2, 1):
        upper = (block & step) != 0
        for a in range(8):
            if a & step:
                continue
            b = a | step
            low, high = parts[a], parts[b]
            parts[a] = jnp.where(upper, pltpu.roll(high, step * PAD, 1), low)
            parts[b] = jnp.where(upper, high, pltpu.roll(low, 128 - step * PAD, 1))
    return parts


def as_column(row):
    return jnp.broadcast_to(row, (C, C)).T[:, :1]


def padded_rows(tile, scratch):
    tile = tile.astype(f32)
    for i in range(PAD):
        part = tile[i] if i < TI else jnp.zeros((TK, C), f32)
        scratch[pl.ds(i, TK, stride=PAD), :] = part
    return scratch[...]


def unpadded_rows(values, scratch):
    scratch[...] = values
    return jnp.stack([scratch[pl.ds(i, TK, stride=PAD), :] for i in range(TI)]).astype(bf16)


def parts_of(slots):
    kinds = slots.shape[1] // C
    step = HELD * kinds
    return [
        jnp.concatenate(
            [
                slots[t, pl.ds(step * R * e + kinds * held + kind, R, stride=step), :]
                for kind in range(kinds)
                for t in range(3)
            ],
            axis=0,
        )
        for held in range(HELD)
        for e in range(E)
    ]


def pack_rows(values):
    spare = lax.broadcasted_iota(jnp.int32, (PACK, 128), 1) % PAD >= TI
    last = values[PACK:]
    moved = [pltpu.roll(last, TI - (PAD - TI) * g, 1) for g in range(3)]
    return jnp.where(spare, jnp.concatenate(moved, axis=0), values[:PACK])


def unpack_rows(packed):
    lane = lax.broadcasted_iota(jnp.int32, (GROUP, 128), 1) % PAD
    last = jnp.zeros((GROUP, 128), f32)
    for g in range(3):
        back = pltpu.roll(packed[GROUP * g : GROUP * (g + 1)], 128 - TI + (PAD - TI) * g, 1)
        last = jnp.where(lane // (PAD - TI) == g, back, last)
    spare = lax.broadcasted_iota(jnp.int32, (PACK, 128), 1) % PAD >= TI
    return jnp.concatenate([jnp.where(spare, 0.0, packed), last], axis=0)


def own_block(shape):
    return lax.broadcasted_iota(jnp.int32, shape, 1) // WIDTH


def norm_rows(values):
    centered = values - jnp.mean(values, axis=1, keepdims=True)
    inv_std = lax.rsqrt(jnp.mean(centered * centered, axis=1, keepdims=True) + norm_eps)
    return centered * inv_std, inv_std


def put_rows(slots, rows, values):
    for t in range(3):
        slots[t, rows, :] = values[:, 128 * t : 128 * (t + 1)]


def get_rows(slots, rows):
    return jnp.concatenate([slots[t, rows, :] for t in range(3)], axis=1)


def message_rows(slots):
    rows = get_rows(slots, slice(None))
    return rows.reshape(C // HELD, rows.shape[0] * HELD // C, LANES).astype(bf16)


def own_rows(slots, received):
    put_rows(slots, slice(None), received[...].astype(f32).reshape(-1, LANES))


def project_kernel(
    crop, pair_hbm, gain_hbm, bias_hbm, weights_hbm, out_gain_hbm, out_bias_hbm,
    send, projected, inside, vectors,
    padded, slots, pair, weights, gain, bias, out_gain, out_bias, arrived,
):
    sources = (pair_hbm, gain_hbm, bias_hbm, weights_hbm, out_gain_hbm, out_bias_hbm)
    targets = (pair, gain, bias, weights, out_gain, out_bias)
    loads = [
        pltpu.make_async_copy(source, target, arrived.at[n])
        for n, (source, target) in enumerate(zip(sources, targets))
    ]
    for load in loads:
        load.start()
    row_pos = lax.axis_index(ROWS)
    col_pos = lax.axis_index(COLS)
    lane = lax.broadcasted_iota(jnp.int32, (8, LANES), 1)
    crop_rows = jnp.zeros((8, LANES), jnp.int32)
    crop_cols = jnp.full((8, LANES), -1, jnp.int32)
    for k in range(TK):
        crop_rows = jnp.where(lane // PAD == k, crop[row_pos * TK + k], crop_rows)
    for i in range(TI):
        crop_cols = jnp.where(lane % PAD == i, crop[col_pos * TI + i], crop_cols)
    same = (crop_rows == crop_cols).astype(f32)
    inside[...] = same
    mask = same[:1, :]

    for load in loads[:3]:
        load.wait()
    hat, _ = norm_rows(padded_rows(pair[...], padded))
    normed = (hat * gain[...] + bias[...]).astype(bf16)
    for load in loads[3:]:
        load.wait()
    vectors[...] = jnp.concatenate(
        [jnp.broadcast_to(v[...], (8, C)) for v in (gain, out_gain, out_bias)], axis=0
    )
    proj = dot(weights[...].T, normed, ((1,), (1,)))
    projected[...] = proj
    left = mask * jax.nn.sigmoid(proj[2 * C : 3 * C]) * proj[:C]
    right = mask * jax.nn.sigmoid(proj[3 * C : 4 * C]) * proj[C : 2 * C]
    put_rows(slots, pl.ds(0, C, stride=2), left)
    put_rows(slots, pl.ds(1, C, stride=2), right)
    send[...] = message_rows(slots)


def collect_kernel(received, left, right, slots):
    own_rows(slots, received)
    parts = parts_of(slots)
    parts = swap_blocks(parts)
    for side, out in enumerate((left, right)):
        pieces = []
        for t in range(3):
            for k in range(8):
                at = (3 * side + t) * R
                pieces.append(parts[k][at : at + RF] + parts[k][at + RF : at + R])
        whole = jnp.concatenate(pieces, axis=0)
        if side:
            out[...] = whole.astype(bf16)
        else:
            packed = pack_rows(whole).astype(bf16)
            for q in range(Q):
                out[q] = packed


def reorder(transposed):
    shape = (N, Q * WIDTH) if transposed else (Q * WIDTH, N)
    wide = lax.broadcasted_iota(jnp.int32, shape, 1 if transposed else 0)
    target = lax.broadcasted_iota(jnp.int32, shape, 0 if transposed else 1)
    within = (wide // PAD % 2) * TI + wide % PAD
    position = wide // (2 * PAD)
    hit = (target == within * R + position) & (wide % PAD < TI)
    return hit.astype(f32).astype(bf16)


def triangle_kernel(left_packed, right, left_all, send, slots):
    for q in range(Q):
        left_all[q] = unpack_rows(left_packed[q].astype(f32)).astype(bf16)
    rows = []
    block = own_block((WIDTH, 128))
    for q in range(Q):
        product = dot(left_all[q], right[...], ((0,), (0,)))
        own = product[:WIDTH]
        for held in range(1, HELD):
            own = jnp.where(block == held, product[WIDTH * held : WIDTH * (held + 1)], own)
        rows.append(own)
    tri = jnp.concatenate(rows, axis=0).astype(bf16)
    tri = dot(reorder(True), tri, ((1,), (0,)))
    parts = [
        jnp.concatenate([tri[(8 * t + i) * R : (8 * t + i + 1) * R] for t in range(3)], axis=0)
        for i in range(8)
    ]
    parts = swap_blocks(parts)
    for held in range(HELD):
        for e in range(E):
            rows = pl.ds(HELD * R * e + held, R, stride=HELD)
            part = parts[held * E + e]
            for t in range(3):
                slots[t, rows, :] = part[t * R : (t + 1) * R]
    send[...] = message_rows(slots)


def output_kernel(
    received, projected, inside, vectors, cotangent, weights, update, d_outpre, send, padded, slots
):
    mask = inside[:1, :]
    own_rows(slots, received)
    tri = jnp.where(mask > 0, get_rows(slots, slice(None)), 0.0)
    centered = tri - jnp.mean(tri, axis=0, keepdims=True)
    inv_out = lax.rsqrt(jnp.mean(centered * centered, axis=0, keepdims=True) + norm_eps)
    tri_hat = centered * inv_out
    gain_col = as_column(vectors[8:9])
    normed_out = (tri_hat * gain_col + as_column(vectors[16:17])).astype(bf16)
    gated_value = dot(weights[...].T, normed_out, ((1,), (0,)))
    gate = jax.nn.sigmoid(projected[4 * C :])
    update[...] = unpadded_rows((gate * gated_value).T, padded)
    upstream = padded_rows(cotangent[...], padded).T
    d_value = (upstream * gate).astype(bf16)
    d_outpre[...] = (upstream * gated_value * gate * (1.0 - gate)).astype(bf16)
    grad = dot(weights[...], d_value, ((1,), (0,))) * gain_col
    first_mean = jnp.mean(grad, axis=0, keepdims=True)
    second_mean = jnp.mean(grad * tri_hat, axis=0, keepdims=True)
    d_tri = inv_out * (grad - first_mean - tri_hat * second_mean)
    put_rows(slots, slice(None), jnp.where(mask > 0, d_tri, 0.0))
    send[...] = message_rows(slots)


def back_kernel(received, left_all, right, d_right, send, slots):
    own_rows(slots, received)
    parts = parts_of(slots)
    parts = swap_blocks(parts)
    d_tri = jnp.concatenate(
        [parts[i][t * R : (t + 1) * R] for t in range(3) for i in range(8)], axis=0
    ).astype(bf16)
    d_tri = dot(reorder(False), d_tri, ((1,), (0,))).astype(bf16)
    total = jnp.zeros((FOLD, 128), f32)
    own = own_block((WIDTH, 128))
    for q in range(Q):
        block = d_tri[WIDTH * q : WIDTH * (q + 1)]
        if HELD > 1:
            block = jnp.concatenate(
                [jnp.where(own == held, block, jnp.zeros_like(block)) for held in range(HELD)],
                axis=0,
            )
        total = total + dot(left_all[q], block, ((1,), (0,)))
        send[q] = pack_rows(dot(right[...], block, ((1,), (1,)))).astype(bf16)
    d_right[...] = total


def spread_kernel(received, d_right, send, slots):
    d_left = received[0].astype(f32)
    for q in range(1, Q):
        d_left = d_left + received[q].astype(f32)
    d_left = unpack_rows(d_left)
    sides = (d_left, d_right[...])
    parts = [
        jnp.concatenate(
            [
                sides[side][(8 * t + k) * RF : (8 * t + k + 1) * RF]
                for side in range(2)
                for t in range(3)
            ],
            axis=0,
        )
        for k in range(8)
    ]
    parts = swap_blocks(parts)
    step = HELD * 2
    for held in range(HELD):
        for e in range(E):
            part = parts[held * E + e]
            for side in range(2):
                for t in range(3):
                    piece = part[(3 * side + t) * RF : (3 * side + t + 1) * RF]
                    for half in range(2):
                        start = step * (R * e + RF * half) + 2 * held + side
                        slots[t, pl.ds(start, RF, stride=step), :] = piece
    send[...] = message_rows(slots)


def input_kernel(
    received, projected, inside, vectors, d_outpre, pair, weights, pair_grad, padded, slots
):
    own_rows(slots, received)
    mask = inside[:1, :]
    d_left = get_rows(slots, pl.ds(0, C, stride=2)) * mask
    d_right = get_rows(slots, pl.ds(1, C, stride=2)) * mask
    left_val, right_val = projected[:C], projected[C : 2 * C]
    left_sig = jax.nn.sigmoid(projected[2 * C : 3 * C])
    right_sig = jax.nn.sigmoid(projected[3 * C : 4 * C])
    d_proj = jnp.concatenate(
        [
            (d_left * left_sig).astype(bf16),
            (d_right * right_sig).astype(bf16),
            (d_left * left_val * left_sig * (1.0 - left_sig)).astype(bf16),
            (d_right * right_val * right_sig * (1.0 - right_sig)).astype(bf16),
            d_outpre[...],
        ],
        axis=0,
    )
    grad = dot(weights[...], d_proj, ((1,), (0,))).T * vectors[:1]
    hat, inv_in = norm_rows(padded_rows(pair[...], padded))
    first_mean = jnp.mean(grad, axis=1, keepdims=True)
    second_mean = jnp.mean(grad * hat, axis=1, keepdims=True)
    pair_grad[...] = unpadded_rows(inv_in * (grad - first_mean - hat * second_mean), padded)


def call(kernel, outs, scratch, *operands, spaces=None, vmem=40):
    spaces = spaces or [pltpu.VMEM] * len(operands)
    return pl.pallas_call(
        kernel,
        out_shape=[jax.ShapeDtypeStruct(shape, dtype) for shape, dtype in outs],
        in_specs=[pl.BlockSpec(memory_space=space) for space in spaces],
        out_specs=[pl.BlockSpec(memory_space=pltpu.VMEM)] * len(outs),
        scratch_shapes=[
            pltpu.VMEM(shape, f32) if isinstance(shape, tuple) else shape for shape in scratch
        ],
        compiler_params=pltpu.CompilerParams(vmem_limit_bytes=vmem * 1024 * 1024),
        name=kernel.__name__,
    )(*operands)


def exchange(messages):
    return lax.all_to_all(messages, OWNERS, 0, 0, tiled=True)


def body(pair, crop, in_gain, in_bias, in_weights, out_gain, out_bias, out_weights, cotangent):
    padded = (LANES, C)
    tile = ((TI, TK, C), bf16)
    pair = pair.transpose(1, 0, 2)
    cotangent = cotangent.transpose(1, 0, 2)
    in_gain, in_bias, out_gain, out_bias = (
        v.reshape(1, C) for v in (in_gain, in_bias, out_gain, out_bias)
    )
    send, projected, inside, vectors = call(
        project_kernel,
        [(BOTH, bf16), ((5 * C, LANES), f32), ((8, LANES), f32), ((24, C), f32)],
        [
            padded, (3, 2 * C, 128), pltpu.VMEM((TI, TK, C), bf16), pltpu.VMEM((C, 5 * C), bf16),
            (1, C), (1, C), (1, C), (1, C), pltpu.SemaphoreType.DMA((6,)),
        ],
        crop, pair, in_gain, in_bias, in_weights, out_gain, out_bias,
        spaces=[pltpu.SMEM] + [pl.ANY] * 6,
        vmem=58,
    )
    left, right = call(
        collect_kernel,
        [((Q, PACK, 128), bf16), ((FOLD, 128), bf16)],
        [(3, 2 * C, 128)],
        exchange(send),
    )
    left = lax.all_to_all(left, "zhi", 0, 0, tiled=True)
    left_all, send = call(
        triangle_kernel,
        [((Q, FOLD, 128), bf16), (ONE, bf16)],
        [(3, C, 128)],
        left, right,
    )
    update, d_outpre, send = call(
        output_kernel,
        [tile, ((C, LANES), bf16), (ONE, bf16)],
        [padded, (3, C, 128)],
        exchange(send), projected, inside, vectors, cotangent, out_weights,
    )
    d_right, send = call(
        back_kernel,
        [((FOLD, 128), f32), ((Q, PACK, 128), bf16)],
        [(3, C, 128)],
        exchange(send), left_all, right,
    )
    partial = lax.all_to_all(send, "zhi", 0, 0, tiled=True)
    (send,) = call(
        spread_kernel, [(BOTH, bf16)], [(3, 2 * C, 128)], partial, d_right
    )
    (pair_grad,) = call(
        input_kernel,
        [tile],
        [padded, (3, 2 * C, 128)],
        exchange(send), projected, inside, vectors, d_outpre, pair, in_weights,
    )
    return update.transpose(1, 0, 2), pair_grad.transpose(1, 0, 2)


def solution(mesh):
    split = Mesh(mesh.devices.reshape(2, 4, 2, Q, 16 // Q, 2), ROWS + COLS)
    tiles = P(ROWS, COLS, None)
    in_specs = (tiles, P(), P(), P(), P(), P(), P(), P(), tiles)
    return jax.shard_map(
        body, mesh=split, in_specs=in_specs, out_specs=(tiles, tiles), check_vma=False
    )
```

```python
import jax
import jax.numpy as jnp
from jax import lax
from jax.experimental import pallas as pl
from jax.experimental.pallas import tpu as pltpu
from jax.sharding import Mesh, PartitionSpec as P

norm_eps = 1e-05
f32 = jnp.float32
bf16 = jnp.bfloat16
ROWS = ("xlo", "y", "core")
COLS = ("zhi", "zlo", "xhi")
OWNERS = ("zlo", "xhi", "xlo", "y", "core")
TK, TI, PAD = 24, 12, 16
LANES = TK * PAD
E, R, Q = 4, 16, 8
HELD = 8 // E
WIDTH = 128 // HELD
C = 128
N = 384
FOLD = N // 2
PACK = FOLD * TI // PAD
GROUP = FOLD - PACK
RF = R // 2
BOTH = (C // HELD, 2 * HELD, LANES)
ONE = (C // HELD, HELD, LANES)


def dot(first_op, second_op, dims):
    return lax.dot_general(first_op, second_op, (dims, ((), ())), preferred_element_type=f32)


def swap_blocks(parts):
    parts = list(parts)
    block = lax.broadcasted_iota(jnp.int32, parts[0].shape, 1) // PAD
    for step in (4, 2, 1):
        upper = (block & step) != 0
        for a in range(8):
            if a & step:
                continue
            b = a | step
            low, high = parts[a], parts[b]
            parts[a] = jnp.where(upper, pltpu.roll(high, step * PAD, 1), low)
            parts[b] = jnp.where(upper, high, pltpu.roll(low, 128 - step * PAD, 1))
    return parts


def as_column(row):
    return jnp.broadcast_to(row, (C, C)).T[:, :1]


def padded_rows(tile, scratch):
    tile = tile.astype(f32)
    for i in range(PAD):
        part = tile[i] if i < TI else jnp.zeros((TK, C), f32)
        scratch[pl.ds(i, TK, stride=PAD), :] = part
    return scratch[...]


def unpadded_rows(values, scratch):
    scratch[...] = values
    return jnp.stack([scratch[pl.ds(i, TK, stride=PAD), :] for i in range(TI)]).astype(bf16)


def parts_of(slots):
    kinds = slots.shape[1] // C
    step = HELD * kinds
    return [
        jnp.concatenate(
            [
                slots[t, pl.ds(step * R * e + kinds * held + kind, R, stride=step), :]
                for kind in range(kinds)
                for t in range(3)
            ],
            axis=0,
        )
        for held in range(HELD)
        for e in range(E)
    ]


def pack_rows(values):
    spare = lax.broadcasted_iota(jnp.int32, (PACK, 128), 1) % PAD >= TI
    last = values[PACK:]
    moved = [pltpu.roll(last, TI - (PAD - TI) * g, 1) for g in range(3)]
    return jnp.where(spare, jnp.concatenate(moved, axis=0), values[:PACK])


def unpack_rows(packed):
    lane = lax.broadcasted_iota(jnp.int32, (GROUP, 128), 1) % PAD
    last = jnp.zeros((GROUP, 128), f32)
    for g in range(3):
        back = pltpu.roll(packed[GROUP * g : GROUP * (g + 1)], 128 - TI + (PAD - TI) * g, 1)
        last = jnp.where(lane // (PAD - TI) == g, back, last)
    spare = lax.broadcasted_iota(jnp.int32, (PACK, 128), 1) % PAD >= TI
    return jnp.concatenate([jnp.where(spare, 0.0, packed), last], axis=0)


def own_block(shape):
    return lax.broadcasted_iota(jnp.int32, shape, 1) // WIDTH


def norm_rows(values):
    centered = values - jnp.mean(values, axis=1, keepdims=True)
    inv_std = lax.rsqrt(jnp.mean(centered * centered, axis=1, keepdims=True) + norm_eps)
    return centered * inv_std, inv_std


def put_rows(slots, rows, values):
    for t in range(3):
        slots[t, rows, :] = values[:, 128 * t : 128 * (t + 1)]


def get_rows(slots, rows):
    return jnp.concatenate([slots[t, rows, :] for t in range(3)], axis=1)


def message_rows(slots):
    rows = get_rows(slots, slice(None))
    return rows.reshape(C // HELD, rows.shape[0] * HELD // C, LANES).astype(bf16)


def own_rows(slots, received):
    put_rows(slots, slice(None), received[...].astype(f32).reshape(-1, LANES))


def project_kernel(
    crop_hbm, pair_hbm, gain_hbm, bias_hbm, weights_hbm, out_gain_hbm, out_bias_hbm,
    send, projected_hbm, inside, vectors,
    padded, slots, projected, crop, pair, gain, bias, weights, out_gain, out_bias, arrived,
):
    sources = (crop_hbm, pair_hbm, gain_hbm, bias_hbm, weights_hbm, out_gain_hbm, out_bias_hbm)
    targets = (crop, pair, gain, bias, weights, out_gain, out_bias)
    loads = [
        pltpu.make_async_copy(source, target, arrived.at[n])
        for n, (source, target) in enumerate(zip(sources, targets))
    ]
    for load in loads:
        load.start()
    loads[1].wait()
    hat, _ = norm_rows(padded_rows(pair[...], padded))
    loads[2].wait()
    loads[3].wait()
    normed = (hat * gain[...] + bias[...]).astype(bf16)
    loads[4].wait()
    projected[...] = dot(weights[...].T, normed, ((1,), (1,)))
    keep = pltpu.make_async_copy(projected, projected_hbm, arrived.at[7])
    keep.start()

    loads[0].wait()
    row_pos = lax.axis_index(ROWS)
    col_pos = lax.axis_index(COLS)
    lane = lax.broadcasted_iota(jnp.int32, (8, LANES), 1)
    crop_rows = jnp.zeros((8, LANES), jnp.int32)
    crop_cols = jnp.full((8, LANES), -1, jnp.int32)
    for k in range(TK):
        crop_rows = jnp.where(lane // PAD == k, crop[row_pos * TK + k], crop_rows)
    for i in range(TI):
        crop_cols = jnp.where(lane % PAD == i, crop[col_pos * TI + i], crop_cols)
    same = (crop_rows == crop_cols).astype(f32)
    inside[...] = same
    mask = same[:1, :]
    left = mask * jax.nn.sigmoid(projected[2 * C : 3 * C]) * projected[:C]
    right = mask * jax.nn.sigmoid(projected[3 * C : 4 * C]) * projected[C : 2 * C]
    put_rows(slots, pl.ds(0, C, stride=2), left)
    put_rows(slots, pl.ds(1, C, stride=2), right)
    send[...] = message_rows(slots)
    loads[5].wait()
    loads[6].wait()
    vectors[...] = jnp.concatenate(
        [jnp.broadcast_to(v[...], (8, C)) for v in (gain, out_gain, out_bias)], axis=0
    )
    keep.wait()


def collect_kernel(received, both, right, slots):
    own_rows(slots, received)
    parts = parts_of(slots)
    parts = swap_blocks(parts)
    for side in range(2):
        pieces = []
        for t in range(3):
            for k in range(8):
                at = (3 * side + t) * R
                pieces.append(parts[k][at : at + RF] + parts[k][at + RF : at + R])
        whole = jnp.concatenate(pieces, axis=0)
        both[PACK * side : PACK * (side + 1)] = pack_rows(whole).astype(bf16)
    right[...] = whole.astype(bf16)


def residue_rows(column):
    return pl.ds(column % 2 * TI * R + column // 2, TI, stride=R)


def triangle_kernel(both, right, left_all, send, slots, ordered):
    block = own_block((WIDTH, 128))
    for q in range(Q):
        left = unpack_rows(both[q, :PACK].astype(f32)).astype(bf16)
        left_all[q] = left
        product = dot(left, right[...], ((0,), (0,)))
        own = product[:WIDTH]
        for held in range(1, HELD):
            own = jnp.where(block == held, product[WIDTH * held : WIDTH * (held + 1)], own)
        for e in range(E):
            ordered[residue_rows(E * q + e), :] = own[PAD * e : PAD * e + TI]
    tri = ordered[...]
    parts = [
        jnp.concatenate([tri[(8 * t + i) * R : (8 * t + i + 1) * R] for t in range(3)], axis=0)
        for i in range(8)
    ]
    parts = swap_blocks(parts)
    for held in range(HELD):
        for e in range(E):
            rows = pl.ds(HELD * R * e + held, R, stride=HELD)
            part = parts[held * E + e]
            for t in range(3):
                slots[t, rows, :] = part[t * R : (t + 1) * R]
    send[...] = message_rows(slots)


def output_kernel(
    received, projected, inside, vectors, cotangent, weights, update_hbm, d_outpre, send,
    padded, slots, update, written,
):
    mask = inside[:1, :]
    own_rows(slots, received)
    tri = jnp.where(mask > 0, get_rows(slots, slice(None)), 0.0)
    centered = tri - jnp.mean(tri, axis=0, keepdims=True)
    inv_out = lax.rsqrt(jnp.mean(centered * centered, axis=0, keepdims=True) + norm_eps)
    tri_hat = centered * inv_out
    gain_col = as_column(vectors[8:9])
    normed_out = (tri_hat * gain_col + as_column(vectors[16:17])).astype(bf16)
    gated_value = dot(weights[...].T, normed_out, ((1,), (0,)))
    gate = jax.nn.sigmoid(projected[4 * C :])
    update[...] = unpadded_rows((gate * gated_value).T, padded)
    write = pltpu.make_async_copy(update, update_hbm, written)
    write.start()
    upstream = padded_rows(cotangent[...], padded).T
    d_value = (upstream * gate).astype(bf16)
    d_outpre[...] = (upstream * gated_value * gate * (1.0 - gate)).astype(bf16)
    grad = dot(weights[...], d_value, ((1,), (0,))) * gain_col
    first_mean = jnp.mean(grad, axis=0, keepdims=True)
    second_mean = jnp.mean(grad * tri_hat, axis=0, keepdims=True)
    d_tri = inv_out * (grad - first_mean - tri_hat * second_mean)
    put_rows(slots, slice(None), jnp.where(mask > 0, d_tri, 0.0))
    send[...] = message_rows(slots)
    write.wait()


def padded_columns(rows):
    spare = jnp.zeros((PAD - TI, 128), f32)
    pieces = []
    for e in range(E):
        pieces += [rows[TI * e : TI * (e + 1)], spare]
    block = jnp.concatenate(pieces, axis=0)
    own = own_block((WIDTH, 128))
    return jnp.concatenate(
        [jnp.where(own == held, block, 0.0) for held in range(HELD)], axis=0
    ).astype(bf16)


def back_kernel(received, left_all, d_right, send, slots, ordered):
    own_rows(slots, received)
    parts = swap_blocks(parts_of(slots))
    for t in range(3):
        for i in range(8):
            ordered[pl.ds((8 * t + i) * R, R), :] = parts[i][t * R : (t + 1) * R]
    total = jnp.zeros((FOLD, 128), f32)
    for q in range(Q):
        rows = jnp.concatenate(
            [ordered[residue_rows(E * q + e), :] for e in range(E)], axis=0
        )
        send[q] = rows.astype(bf16)
        total = total + dot(left_all[q], padded_columns(rows), ((1,), (0,)))
    d_right[...] = total


def spread_kernel(received, both, d_right, send, slots):
    d_left = jnp.zeros((FOLD, 128), f32)
    for q in range(Q):
        right = unpack_rows(both[q, PACK:].astype(f32)).astype(bf16)
        rows = padded_columns(received[q].astype(f32))
        d_left = d_left + dot(right, rows, ((1,), (1,)))
    sides = (d_left, d_right[...])
    parts = [
        jnp.concatenate(
            [
                sides[side][(8 * t + k) * RF : (8 * t + k + 1) * RF]
                for side in range(2)
                for t in range(3)
            ],
            axis=0,
        )
        for k in range(8)
    ]
    parts = swap_blocks(parts)
    step = HELD * 2
    for held in range(HELD):
        for e in range(E):
            part = parts[held * E + e]
            for side in range(2):
                for t in range(3):
                    piece = part[(3 * side + t) * RF : (3 * side + t + 1) * RF]
                    for half in range(2):
                        start = step * (R * e + RF * half) + 2 * held + side
                        slots[t, pl.ds(start, RF, stride=step), :] = piece
    send[...] = message_rows(slots)


def input_kernel(
    received, projected, inside, vectors, d_outpre, pair, weights, pair_grad, padded, slots
):
    own_rows(slots, received)
    mask = inside[:1, :]
    d_left = get_rows(slots, pl.ds(0, C, stride=2)) * mask
    d_right = get_rows(slots, pl.ds(1, C, stride=2)) * mask
    left_val, right_val = projected[:C], projected[C : 2 * C]
    left_sig = jax.nn.sigmoid(projected[2 * C : 3 * C])
    right_sig = jax.nn.sigmoid(projected[3 * C : 4 * C])
    d_proj = jnp.concatenate(
        [
            (d_left * left_sig).astype(bf16),
            (d_right * right_sig).astype(bf16),
            (d_left * left_val * left_sig * (1.0 - left_sig)).astype(bf16),
            (d_right * right_val * right_sig * (1.0 - right_sig)).astype(bf16),
            d_outpre[...],
        ],
        axis=0,
    )
    grad = dot(weights[...], d_proj, ((1,), (0,))).T * vectors[:1]
    hat, inv_in = norm_rows(padded_rows(pair[...], padded))
    first_mean = jnp.mean(grad, axis=1, keepdims=True)
    second_mean = jnp.mean(grad * hat, axis=1, keepdims=True)
    pair_grad[...] = unpadded_rows(inv_in * (grad - first_mean - hat * second_mean), padded)


def call(kernel, outs, scratch, *operands, inputs=None, written=(), vmem=40):
    inputs = inputs or [pltpu.VMEM] * len(operands)
    return pl.pallas_call(
        kernel,
        out_shape=[jax.ShapeDtypeStruct(shape, dtype) for shape, dtype in outs],
        in_specs=[pl.BlockSpec(memory_space=space) for space in inputs],
        out_specs=[
            pl.BlockSpec(memory_space=pl.ANY if n in written else pltpu.VMEM)
            for n in range(len(outs))
        ],
        scratch_shapes=[
            pltpu.VMEM(shape, f32) if isinstance(shape, tuple) else shape for shape in scratch
        ],
        compiler_params=pltpu.CompilerParams(vmem_limit_bytes=vmem * 1024 * 1024),
        name=kernel.__name__,
    )(*operands)


def exchange(messages):
    return lax.all_to_all(messages, OWNERS, 0, 0, tiled=True)


def body(pair, crop, in_gain, in_bias, in_weights, out_gain, out_bias, out_weights, cotangent):
    padded = (LANES, C)
    tile = ((TI, TK, C), bf16)
    pair = pair.transpose(1, 0, 2)
    cotangent = cotangent.transpose(1, 0, 2)
    in_gain, in_bias, out_gain, out_bias = (
        v.reshape(1, C) for v in (in_gain, in_bias, out_gain, out_bias)
    )
    send, projected, inside, vectors = call(
        project_kernel,
        [(BOTH, bf16), ((5 * C, LANES), f32), ((8, LANES), f32), ((24, C), f32)],
        [
            padded, (3, 2 * C, 128), (5 * C, LANES), pltpu.SMEM((N,), jnp.int32),
            pltpu.VMEM((TI, TK, C), bf16), (1, C), (1, C), pltpu.VMEM((C, 5 * C), bf16),
            (1, C), (1, C), pltpu.SemaphoreType.DMA((8,)),
        ],
        crop, pair, in_gain, in_bias, in_weights, out_gain, out_bias,
        inputs=[pl.ANY] * 7,
        written=(1,),
        vmem=58,
    )
    both, right = call(
        collect_kernel,
        [((2 * PACK, 128), bf16), ((FOLD, 128), bf16)],
        [(3, 2 * C, 128)],
        exchange(send),
    )
    both = lax.all_gather(both, "zhi", axis=0)
    left_all, send = call(
        triangle_kernel,
        [((Q, FOLD, 128), bf16), (ONE, bf16)],
        [(3, C, 128), (N, 128)],
        both, right,
    )
    update, d_outpre, send = call(
        output_kernel,
        [tile, ((C, LANES), bf16), (ONE, bf16)],
        [padded, (3, C, 128), pltpu.VMEM((TI, TK, C), bf16), pltpu.SemaphoreType.DMA(())],
        exchange(send), projected, inside, vectors, cotangent, out_weights,
        written=(0,),
    )
    d_right, send = call(
        back_kernel,
        [((FOLD, 128), f32), ((Q, E * TI, 128), bf16)],
        [(3, C, 128), (N, 128)],
        exchange(send), left_all,
    )
    rows = lax.all_to_all(send, "zhi", 0, 0, tiled=True)
    (send,) = call(
        spread_kernel, [(BOTH, bf16)], [(3, 2 * C, 128)], rows, both, d_right
    )
    (pair_grad,) = call(
        input_kernel,
        [tile],
        [padded, (3, 2 * C, 128)],
        exchange(send), projected, inside, vectors, d_outpre, pair, in_weights,
    )
    return update.transpose(1, 0, 2), pair_grad.transpose(1, 0, 2)


def solution(mesh):
    split = Mesh(mesh.devices.reshape(2, 4, 2, Q, 16 // Q, 2), ROWS + COLS)
    tiles = P(ROWS, COLS, None)
    in_specs = (tiles, P(), P(), P(), P(), P(), P(), P(), tiles)
    return jax.shard_map(
        body, mesh=split, in_specs=in_specs, out_specs=(tiles, tiles), check_vma=False
    )
```

```python
import jax
import jax.numpy as jnp
from jax import lax
from jax.experimental import pallas as pl
from jax.experimental.pallas import tpu as pltpu
from jax.sharding import Mesh, PartitionSpec as P

norm_eps = 1e-05
f32 = jnp.float32
bf16 = jnp.bfloat16
ROWS = ("xlo", "y", "core")
COLS = ("zhi", "zlo", "xhi")
OWNERS = ("zlo", "xhi", "xlo", "y", "core")
TK, TI, PAD = 24, 12, 16
LANES = TK * PAD
E, R, Q = 4, 16, 8
HELD = 8 // E
WIDTH = 128 // HELD
C = 128
N = 384
FOLD = N // 2
PACK = FOLD * TI // PAD
GROUP = FOLD - PACK
RF = R // 2


def dot(first_op, second_op, dims):
    return lax.dot_general(first_op, second_op, (dims, ((), ())), preferred_element_type=f32)


def swap_blocks(parts):
    parts = list(parts)
    block = lax.broadcasted_iota(jnp.int32, parts[0].shape, 1) // PAD
    for step in (4, 2, 1):
        upper = (block & step) != 0
        for a in range(8):
            if a & step:
                continue
            b = a | step
            low, high = parts[a], parts[b]
            parts[a] = jnp.where(upper, pltpu.roll(high, step * PAD, 1), low)
            parts[b] = jnp.where(upper, high, pltpu.roll(low, 128 - step * PAD, 1))
    return parts


def as_column(row):
    return jnp.broadcast_to(row, (C, C)).T[:, :1]


def padded_rows(tile, scratch):
    tile = tile.astype(f32)
    for i in range(PAD):
        part = tile[i] if i < TI else jnp.zeros((TK, C), f32)
        scratch[pl.ds(i, TK, stride=PAD), :] = part
    return scratch[...]


def unpadded_rows(values, scratch):
    scratch[...] = values
    return jnp.stack([scratch[pl.ds(i, TK, stride=PAD), :] for i in range(TI)]).astype(bf16)


def parts_of(slots):
    return [
        jnp.concatenate([slots[n, from_owner(held, e), :] for n in range(slots.shape[0])], axis=0)
        for held in range(HELD)
        for e in range(E)
    ]


def pack_rows(values):
    spare = lax.broadcasted_iota(jnp.int32, (PACK, 128), 1) % PAD >= TI
    last = values[PACK:]
    moved = [pltpu.roll(last, TI - (PAD - TI) * g, 1) for g in range(3)]
    return jnp.where(spare, jnp.concatenate(moved, axis=0), values[:PACK])


def unpack_rows(packed):
    lane = lax.broadcasted_iota(jnp.int32, (GROUP, 128), 1) % PAD
    last = jnp.zeros((GROUP, 128), f32)
    for g in range(3):
        back = pltpu.roll(packed[GROUP * g : GROUP * (g + 1)], 128 - TI + (PAD - TI) * g, 1)
        last = jnp.where(lane // (PAD - TI) == g, back, last)
    spare = lax.broadcasted_iota(jnp.int32, (PACK, 128), 1) % PAD >= TI
    return jnp.concatenate([jnp.where(spare, 0.0, packed), last], axis=0)


def own_block(shape):
    return lax.broadcasted_iota(jnp.int32, shape, 1) // WIDTH


def norm_rows(values):
    centered = values - jnp.mean(values, axis=1, keepdims=True)
    inv_std = lax.rsqrt(jnp.mean(centered * centered, axis=1, keepdims=True) + norm_eps)
    return centered * inv_std, inv_std


def put_kind(slots, kind, values):
    for t in range(3):
        slots[3 * kind + t, :, :] = values[:, 128 * t : 128 * (t + 1)]


def get_kind(slots, kind):
    return jnp.concatenate([slots[3 * kind + t, :, :] for t in range(3)], axis=1)


def as_messages(slots):
    rows = jnp.concatenate([slots[n, :, :] for n in range(slots.shape[0])], axis=1)
    return rows.reshape(C // HELD, HELD, -1).astype(bf16)


def from_messages(slots, received):
    rows = received[...].astype(f32).reshape(C, -1)
    for n in range(slots.shape[0]):
        slots[n, :, :] = rows[:, 128 * n : 128 * (n + 1)]


def from_owner(held, e):
    return pl.ds(HELD * R * e + held, R, stride=HELD)


def project_kernel(
    crop_hbm, pair_hbm, gain_hbm, bias_hbm, weights_hbm, out_gain_hbm, out_bias_hbm,
    cotangent_hbm, out_weights_hbm, send, projected_hbm, inside, vectors, grad,
    padded, slots, projected, crop, pair, gain, bias, weights, out_gain, out_bias,
    cotangent, out_weights, arrived,
):
    sources = (
        crop_hbm, pair_hbm, gain_hbm, bias_hbm, weights_hbm, out_gain_hbm, out_bias_hbm,
        cotangent_hbm, out_weights_hbm,
    )
    targets = (crop, pair, gain, bias, weights, out_gain, out_bias, cotangent, out_weights)
    loads = [
        pltpu.make_async_copy(source, target, arrived.at[n])
        for n, (source, target) in enumerate(zip(sources, targets))
    ]
    for load in loads:
        load.start()
    loads[1].wait()
    hat, _ = norm_rows(padded_rows(pair[...], padded))
    loads[2].wait()
    loads[3].wait()
    normed = (hat * gain[...] + bias[...]).astype(bf16)
    loads[4].wait()
    projected[...] = dot(weights[...].T, normed, ((1,), (1,)))
    keep = pltpu.make_async_copy(projected, projected_hbm, arrived.at[9])
    keep.start()

    loads[0].wait()
    row_pos = lax.axis_index(ROWS)
    col_pos = lax.axis_index(COLS)
    lane = lax.broadcasted_iota(jnp.int32, (8, LANES), 1)
    crop_rows = jnp.zeros((8, LANES), jnp.int32)
    crop_cols = jnp.full((8, LANES), -1, jnp.int32)
    for k in range(TK):
        crop_rows = jnp.where(lane // PAD == k, crop[row_pos * TK + k], crop_rows)
    for i in range(TI):
        crop_cols = jnp.where(lane % PAD == i, crop[col_pos * TI + i], crop_cols)
    same = (crop_rows == crop_cols).astype(f32)
    inside[...] = same
    mask = same[:1, :]
    put_kind(slots, 0, mask * jax.nn.sigmoid(projected[2 * C : 3 * C]) * projected[:C])
    put_kind(slots, 1, mask * jax.nn.sigmoid(projected[3 * C : 4 * C]) * projected[C : 2 * C])
    for load in loads[5:]:
        load.wait()
    upstream = padded_rows(cotangent[...], padded).T
    d_value = (upstream * jax.nn.sigmoid(projected[4 * C :])).astype(bf16)
    value_grad = dot(out_weights[...], d_value, ((1,), (0,))) * as_column(out_gain[...])
    grad[...] = value_grad
    put_kind(slots, 2, jnp.where(mask > 0, value_grad, 0.0))
    send[...] = as_messages(slots)
    vectors[...] = jnp.concatenate(
        [jnp.broadcast_to(v[...], (8, C)) for v in (gain, out_gain, out_bias)], axis=0
    )
    keep.wait()


def collect_kernel(received, gathered, left, right, slots):
    from_messages(slots, received)
    parts = swap_blocks(parts_of(slots))
    for kind in range(3):
        pieces = []
        for t in range(3):
            for k in range(8):
                at = (3 * kind + t) * R
                pieces.append(parts[k][at : at + RF] + parts[k][at + RF : at + R])
        whole = jnp.concatenate(pieces, axis=0)
        gathered[PACK * kind : PACK * (kind + 1)] = pack_rows(whole).astype(bf16)
        if kind < 2:
            (left, right)[kind][...] = whole.astype(bf16)


def residue_rows(column):
    return pl.ds(column % 2 * TI * R + column // 2, TI, stride=R)


def own_rows(block):
    lanes = own_block((WIDTH, 128))
    own = block[:WIDTH]
    for held in range(1, HELD):
        own = jnp.where(lanes == held, block[WIDTH * held : WIDTH * (held + 1)], own)
    return own


def triangle_kernel(gathered, left, right, left_all, right_all, send, slots, ordered, folded):
    place = 2 * (lax.axis_index("zhi") % (Q // 2))
    spare = jnp.zeros((PAD - TI, 128), f32)
    for q in range(Q):
        left_q = unpack_rows(gathered[q, :PACK].astype(f32)).astype(bf16)
        right_q = unpack_rows(gathered[q, PACK : 2 * PACK].astype(f32)).astype(bf16)
        left_all[q] = left_q
        right_all[q] = right_q
        folded[...] = unpack_rows(gathered[q, 2 * PACK :].astype(f32))
        own_i = [folded[pl.ds(place + half, TK, stride=RF), :] for half in range(2)]
        pieces = []
        for e in range(E):
            pieces += [own_i[e // 2][e % 2 * TI : (e % 2 + 1) * TI], spare]
        blocks = (
            dot(left_q, right[...], ((0,), (0,))),
            dot(right_q, left[...], ((0,), (0,))),
            jnp.concatenate(pieces * HELD, axis=0).T,
        )
        for kind, block in enumerate(blocks):
            own = own_rows(block)
            for e in range(E):
                ordered[kind, residue_rows(E * q + e), :] = own[PAD * e : PAD * e + TI]
    parts = swap_blocks(
        [
            jnp.concatenate(
                [ordered[kind, (8 * t + i) * R : (8 * t + i + 1) * R] for kind in range(3) for t in range(3)],
                axis=0,
            )
            for i in range(8)
        ]
    )
    for held in range(HELD):
        for e in range(E):
            part = parts[held * E + e]
            for n in range(9):
                slots[n, from_owner(held, e), :] = part[n * R : (n + 1) * R]
    send[...] = as_messages(slots)


def norm_tri(slots, kind, mask):
    tri = jnp.where(mask, get_kind(slots, kind), 0.0)
    centered = tri - jnp.mean(tri, axis=0, keepdims=True)
    inv_out = lax.rsqrt(jnp.mean(centered * centered, axis=0, keepdims=True) + norm_eps)
    return centered * inv_out, inv_out


def norm_back(grad, tri_hat, inv_out, mask):
    first_mean = jnp.mean(grad, axis=0, keepdims=True)
    second_mean = jnp.mean(grad * tri_hat, axis=0, keepdims=True)
    return jnp.where(mask, inv_out * (grad - first_mean - tri_hat * second_mean), 0.0)


def output_kernel(
    received, projected, inside, vectors, grad, cotangent, weights, update_hbm, d_outpre, send,
    padded, slots, slots_back, update, written,
):
    mask = inside[:1, :] > 0
    from_messages(slots, received)
    tri_hat, inv_out = norm_tri(slots, 0, mask)
    normed_out = (tri_hat * as_column(vectors[8:9]) + as_column(vectors[16:17])).astype(bf16)
    gated_value = dot(weights[...].T, normed_out, ((1,), (0,)))
    gate = jax.nn.sigmoid(projected[4 * C :])
    update[...] = unpadded_rows((gate * gated_value).T, padded)
    write = pltpu.make_async_copy(update, update_hbm, written)
    write.start()
    put_kind(slots_back, 0, norm_back(grad[...], tri_hat, inv_out, mask))
    mirror_hat, mirror_inv = norm_tri(slots, 1, mask)
    mirror_grad = jnp.where(mask, get_kind(slots, 2), 0.0)
    put_kind(slots_back, 1, norm_back(mirror_grad, mirror_hat, mirror_inv, mask))
    send[...] = as_messages(slots_back)
    upstream = padded_rows(cotangent[...], padded).T
    d_outpre[...] = (upstream * gated_value * gate * (1.0 - gate)).astype(bf16)
    write.wait()


def padded_columns(rows):
    spare = jnp.zeros((PAD - TI, 128), f32)
    pieces = []
    for e in range(E):
        pieces += [rows[TI * e : TI * (e + 1)], spare]
    block = jnp.concatenate(pieces, axis=0)
    own = own_block((WIDTH, 128))
    return jnp.concatenate(
        [jnp.where(own == held, block, 0.0) for held in range(HELD)], axis=0
    ).astype(bf16)


def back_kernel(received, left_all, right_all, send, slots, ordered):
    from_messages(slots, received)
    parts = swap_blocks(parts_of(slots))
    for kind in range(2):
        for t in range(3):
            for i in range(8):
                n = 3 * kind + t
                ordered[kind, pl.ds((8 * t + i) * R, R), :] = parts[i][n * R : (n + 1) * R]
    d_left = jnp.zeros((FOLD, 128), f32)
    d_right = jnp.zeros((FOLD, 128), f32)
    for q in range(Q):
        by_i, by_j = (
            padded_columns(
                jnp.concatenate([ordered[kind, residue_rows(E * q + e), :] for e in range(E)], axis=0)
            )
            for kind in range(2)
        )
        d_right = d_right + dot(left_all[q], by_i, ((1,), (0,)))
        d_left = d_left + dot(right_all[q], by_j, ((1,), (0,)))
    sides = (d_left, d_right)
    parts = swap_blocks(
        [
            jnp.concatenate(
                [
                    sides[side][(8 * t + k) * RF : (8 * t + k + 1) * RF]
                    for side in range(2)
                    for t in range(3)
                ],
                axis=0,
            )
            for k in range(8)
        ]
    )
    for held in range(HELD):
        for e in range(E):
            part = parts[held * E + e]
            for n in range(6):
                piece = part[n * RF : (n + 1) * RF]
                for half in range(2):
                    start = HELD * (R * e + RF * half) + held
                    slots[n, pl.ds(start, RF, stride=HELD), :] = piece
    send[...] = as_messages(slots)


def input_kernel(
    received, projected, inside, vectors, d_outpre, pair, weights, pair_grad, padded, slots
):
    from_messages(slots, received)
    mask = inside[:1, :]
    d_left = get_kind(slots, 0) * mask
    d_right = get_kind(slots, 1) * mask
    left_val, right_val = projected[:C], projected[C : 2 * C]
    left_sig = jax.nn.sigmoid(projected[2 * C : 3 * C])
    right_sig = jax.nn.sigmoid(projected[3 * C : 4 * C])
    d_proj = jnp.concatenate(
        [
            (d_left * left_sig).astype(bf16),
            (d_right * right_sig).astype(bf16),
            (d_left * left_val * left_sig * (1.0 - left_sig)).astype(bf16),
            (d_right * right_val * right_sig * (1.0 - right_sig)).astype(bf16),
            d_outpre[...],
        ],
        axis=0,
    )
    grad = dot(weights[...], d_proj, ((1,), (0,))).T * vectors[:1]
    hat, inv_in = norm_rows(padded_rows(pair[...], padded))
    first_mean = jnp.mean(grad, axis=1, keepdims=True)
    second_mean = jnp.mean(grad * hat, axis=1, keepdims=True)
    pair_grad[...] = unpadded_rows(inv_in * (grad - first_mean - hat * second_mean), padded)


def call(kernel, outs, scratch, *operands, inputs=None, written=(), vmem=40):
    inputs = inputs or [pltpu.VMEM] * len(operands)
    return pl.pallas_call(
        kernel,
        out_shape=[jax.ShapeDtypeStruct(shape, dtype) for shape, dtype in outs],
        in_specs=[pl.BlockSpec(memory_space=space) for space in inputs],
        out_specs=[
            pl.BlockSpec(memory_space=pl.ANY if n in written else pltpu.VMEM)
            for n in range(len(outs))
        ],
        scratch_shapes=[
            pltpu.VMEM(shape, f32) if isinstance(shape, tuple) else shape for shape in scratch
        ],
        compiler_params=pltpu.CompilerParams(vmem_limit_bytes=vmem * 1024 * 1024),
        name=kernel.__name__,
    )(*operands)


def exchange(messages):
    return lax.all_to_all(messages, OWNERS, 0, 0, tiled=True)


def body(pair, crop, in_gain, in_bias, in_weights, out_gain, out_bias, out_weights, cotangent):
    padded = (LANES, C)
    tile = ((TI, TK, C), bf16)
    pair = pair.transpose(1, 0, 2)
    cotangent = cotangent.transpose(1, 0, 2)
    in_gain, in_bias, out_gain, out_bias = (
        v.reshape(1, C) for v in (in_gain, in_bias, out_gain, out_bias)
    )
    def messages(kinds):
        return ((C // HELD, HELD, kinds * LANES), bf16)

    def slots(kinds):
        return (3 * kinds, C, 128)

    every_block = ((Q, FOLD, 128), bf16)
    own = ((FOLD, 128), bf16)
    send, projected, inside, vectors, grad = call(
        project_kernel,
        [messages(3), ((5 * C, LANES), f32), ((8, LANES), f32), ((24, C), f32), ((C, LANES), f32)],
        [
            padded, slots(3), (5 * C, LANES), pltpu.SMEM((N,), jnp.int32),
            pltpu.VMEM((TI, TK, C), bf16), (1, C), (1, C), pltpu.VMEM((C, 5 * C), bf16),
            (1, C), (1, C), pltpu.VMEM((TI, TK, C), bf16), pltpu.VMEM((C, C), bf16),
            pltpu.SemaphoreType.DMA((10,)),
        ],
        crop, pair, in_gain, in_bias, in_weights, out_gain, out_bias, cotangent, out_weights,
        inputs=[pl.ANY] * 9,
        written=(1,),
        vmem=58,
    )
    gathered, left, right = call(
        collect_kernel,
        [((3 * PACK, 128), bf16), own, own],
        [slots(3)],
        exchange(send),
    )
    left_all, right_all, send = call(
        triangle_kernel,
        [every_block, every_block, messages(3)],
        [slots(3), (3, N, 128), (FOLD, 128)],
        lax.all_gather(gathered, "zhi", axis=0), left, right,
    )
    update, d_outpre, send = call(
        output_kernel,
        [tile, ((C, LANES), bf16), messages(2)],
        [
            padded, slots(3), slots(2), pltpu.VMEM((TI, TK, C), bf16), pltpu.SemaphoreType.DMA(()),
        ],
        exchange(send), projected, inside, vectors, grad, cotangent, out_weights,
        written=(0,),
    )
    (send,) = call(
        back_kernel,
        [messages(2)],
        [slots(2), (2, N, 128)],
        exchange(send), left_all, right_all,
    )
    (pair_grad,) = call(
        input_kernel,
        [tile],
        [padded, slots(2)],
        exchange(send), projected, inside, vectors, d_outpre, pair, in_weights,
    )
    return update.transpose(1, 0, 2), pair_grad.transpose(1, 0, 2)


def solution(mesh):
    split = Mesh(mesh.devices.reshape(2, 4, 2, Q, 16 // Q, 2), ROWS + COLS)
    tiles = P(ROWS, COLS, None)
    in_specs = (tiles, P(), P(), P(), P(), P(), P(), P(), tiles)
    return jax.shard_map(
        body, mesh=split, in_specs=in_specs, out_specs=(tiles, tiles), check_vma=False
    )
```

```python
import jax
import jax.numpy as jnp
from jax import lax
from jax.experimental import pallas as pl
from jax.experimental.pallas import tpu as pltpu
from jax.sharding import Mesh, PartitionSpec as P

norm_eps = 1e-05
f32 = jnp.float32
bf16 = jnp.bfloat16
ROWS = ("xlo", "y", "core")
COLS = ("zhi", "zlo", "xhi")
OWNERS = ("zlo", "xhi", "xlo", "y", "core")
TK, TI, PAD = 24, 12, 16
LANES = TK * PAD
E, R, Q = 4, 16, 8
HELD = 8 // E
WIDTH = 128 // HELD
C = 128
N = 384
FOLD = N // 2
PACK = FOLD * TI // PAD
GROUP = FOLD - PACK
RF = R // 2


def dot(first_op, second_op, dims):
    return lax.dot_general(first_op, second_op, (dims, ((), ())), preferred_element_type=f32)


def swap_blocks(parts):
    parts = list(parts)
    block = lax.broadcasted_iota(jnp.int32, parts[0].shape, 1) // PAD
    for step in (4, 2, 1):
        upper = (block & step) != 0
        for a in range(8):
            if a & step:
                continue
            b = a | step
            low, high = parts[a], parts[b]
            parts[a] = jnp.where(upper, pltpu.roll(high, step * PAD, 1), low)
            parts[b] = jnp.where(upper, high, pltpu.roll(low, 128 - step * PAD, 1))
    return parts


def as_column(row):
    return jnp.broadcast_to(row, (C, C)).T[:, :1]


def padded_rows(tile, scratch):
    tile = tile.astype(f32)
    for i in range(PAD):
        part = tile[i] if i < TI else jnp.zeros((TK, C), f32)
        scratch[pl.ds(i, TK, stride=PAD), :] = part
    return scratch[...]


def unpadded_rows(values, scratch):
    scratch[...] = values
    return jnp.stack([scratch[pl.ds(i, TK, stride=PAD), :] for i in range(TI)]).astype(bf16)


def parts_of(slots, kinds):
    parts = []
    for held in range(HELD):
        for e in range(E):
            packed = [slots[n, from_owner(held, e), :] for n in range(slots.shape[0])]
            parts.append(jnp.concatenate(unpack_slabs(packed, 3 * kinds), axis=0))
    return parts


def pack_rows(values):
    spare = lax.broadcasted_iota(jnp.int32, (PACK, 128), 1) % PAD >= TI
    last = values[PACK:]
    moved = [pltpu.roll(last, TI - (PAD - TI) * g, 1) for g in range(3)]
    return jnp.where(spare, jnp.concatenate(moved, axis=0), values[:PACK])


def unpack_rows(packed):
    lane = lax.broadcasted_iota(jnp.int32, (GROUP, 128), 1) % PAD
    last = jnp.zeros((GROUP, 128), f32)
    for g in range(3):
        back = pltpu.roll(packed[GROUP * g : GROUP * (g + 1)], 128 - TI + (PAD - TI) * g, 1)
        last = jnp.where(lane // (PAD - TI) == g, back, last)
    spare = lax.broadcasted_iota(jnp.int32, (PACK, 128), 1) % PAD >= TI
    return jnp.concatenate([jnp.where(spare, 0.0, packed), last], axis=0)


def own_block(shape):
    return lax.broadcasted_iota(jnp.int32, shape, 1) // WIDTH


def norm_rows(values):
    centered = values - jnp.mean(values, axis=1, keepdims=True)
    inv_std = lax.rsqrt(jnp.mean(centered * centered, axis=1, keepdims=True) + norm_eps)
    return centered * inv_std, inv_std


def slabs_of(values):
    return [values[:, 128 * t : 128 * (t + 1)] for t in range(3)]


def get_kind(slabs, kind):
    return jnp.concatenate(slabs[3 * kind : 3 * kind + 3], axis=1)


def pack_slabs(slabs):
    rest, packed = list(slabs), []
    lane = lax.broadcasted_iota(jnp.int32, rest[0].shape, 1) % PAD
    while len(rest) >= 4:
        for g in range(3):
            moved = pltpu.roll(rest[3], TI - (PAD - TI) * g, 1)
            packed.append(jnp.where(lane >= TI, moved, rest[g]))
        rest = rest[4:]
    return packed + rest


def unpack_slabs(packed, count):
    rest, slabs = list(packed), []
    lane = lax.broadcasted_iota(jnp.int32, rest[0].shape, 1) % PAD
    while count - len(slabs) >= 4:
        back = [pltpu.roll(rest[g], 128 - TI + (PAD - TI) * g, 1) for g in range(3)]
        last = jnp.where(lane < 4, back[0], jnp.where(lane < 8, back[1], back[2]))
        slabs += rest[:3] + [last]
        rest = rest[3:]
    return slabs + rest


def packed_count(kinds):
    return 3 * kinds - 3 * kinds // 4


def as_messages(packed):
    return jnp.concatenate(packed, axis=1).reshape(C // HELD, HELD, -1).astype(bf16)


def from_messages(received):
    rows = received[...].astype(f32).reshape(C, -1)
    return [rows[:, n : n + 128] for n in range(0, rows.shape[1], 128)]


def fill_slots(slots, received):
    for n, slab in enumerate(from_messages(received)):
        slots[n, :, :] = slab


def all_slots(slots):
    return [slots[n, :, :] for n in range(slots.shape[0])]


def from_owner(held, e):
    return pl.ds(HELD * R * e + held, R, stride=HELD)


def project_kernel(
    crop_hbm, pair_hbm, gain_hbm, bias_hbm, weights_hbm, out_gain_hbm, out_bias_hbm,
    cotangent_hbm, out_weights_hbm, send, projected_hbm, inside, vectors, grad,
    padded, projected, crop, pair, gain, bias, weights, out_gain, out_bias,
    cotangent, out_weights, arrived,
):
    sources = (
        crop_hbm, pair_hbm, gain_hbm, bias_hbm, weights_hbm, out_gain_hbm, out_bias_hbm,
        cotangent_hbm, out_weights_hbm,
    )
    targets = (crop, pair, gain, bias, weights, out_gain, out_bias, cotangent, out_weights)
    loads = [
        pltpu.make_async_copy(source, target, arrived.at[n])
        for n, (source, target) in enumerate(zip(sources, targets))
    ]
    for load in loads:
        load.start()
    loads[1].wait()
    hat, _ = norm_rows(padded_rows(pair[...], padded))
    loads[2].wait()
    loads[3].wait()
    normed = (hat * gain[...] + bias[...]).astype(bf16)
    loads[4].wait()
    projected[...] = dot(weights[...].T, normed, ((1,), (1,)))
    keep = pltpu.make_async_copy(projected, projected_hbm, arrived.at[9])
    keep.start()

    loads[0].wait()
    row_pos = lax.axis_index(ROWS)
    col_pos = lax.axis_index(COLS)
    lane = lax.broadcasted_iota(jnp.int32, (8, LANES), 1)
    crop_rows = jnp.zeros((8, LANES), jnp.int32)
    crop_cols = jnp.full((8, LANES), -1, jnp.int32)
    for k in range(TK):
        crop_rows = jnp.where(lane // PAD == k, crop[row_pos * TK + k], crop_rows)
    for i in range(TI):
        crop_cols = jnp.where(lane % PAD == i, crop[col_pos * TI + i], crop_cols)
    same = (crop_rows == crop_cols).astype(f32)
    inside[...] = same
    mask = same[:1, :]
    left = mask * jax.nn.sigmoid(projected[2 * C : 3 * C]) * projected[:C]
    right = mask * jax.nn.sigmoid(projected[3 * C : 4 * C]) * projected[C : 2 * C]
    for load in loads[5:]:
        load.wait()
    upstream = padded_rows(cotangent[...], padded).T
    d_value = (upstream * jax.nn.sigmoid(projected[4 * C :])).astype(bf16)
    value_grad = dot(out_weights[...], d_value, ((1,), (0,))) * as_column(out_gain[...])
    grad[...] = value_grad
    masked_grad = jnp.where(mask > 0, value_grad, 0.0)
    send[...] = as_messages(
        pack_slabs(slabs_of(left) + slabs_of(right) + slabs_of(masked_grad))
    )
    vectors[...] = jnp.concatenate(
        [jnp.broadcast_to(v[...], (8, C)) for v in (gain, out_gain, out_bias)], axis=0
    )
    keep.wait()


def collect_kernel(received, gathered, left, right, slots):
    fill_slots(slots, received)
    parts = swap_blocks(parts_of(slots, 3))
    for kind in range(3):
        pieces = []
        for t in range(3):
            for k in range(8):
                at = (3 * kind + t) * R
                pieces.append(parts[k][at : at + RF] + parts[k][at + RF : at + R])
        whole = jnp.concatenate(pieces, axis=0)
        gathered[PACK * kind : PACK * (kind + 1)] = pack_rows(whole).astype(bf16)
        if kind < 2:
            (left, right)[kind][...] = whole.astype(bf16)


def residue_rows(column):
    return pl.ds(column % 2 * TI * R + column // 2, TI, stride=R)


def own_rows(block):
    lanes = own_block((WIDTH, 128))
    own = block[:WIDTH]
    for held in range(1, HELD):
        own = jnp.where(lanes == held, block[WIDTH * held : WIDTH * (held + 1)], own)
    return own


def triangle_kernel(gathered, left, right, left_all, right_all, send, slots, ordered, folded):
    place = 2 * (lax.axis_index("zhi") % (Q // 2))
    spare = jnp.zeros((PAD - TI, 128), f32)
    for q in range(Q):
        left_q = unpack_rows(gathered[q, :PACK].astype(f32)).astype(bf16)
        right_q = unpack_rows(gathered[q, PACK : 2 * PACK].astype(f32)).astype(bf16)
        left_all[q] = left_q
        right_all[q] = right_q
        folded[...] = unpack_rows(gathered[q, 2 * PACK :].astype(f32))
        own_i = [folded[pl.ds(place + half, TK, stride=RF), :] for half in range(2)]
        pieces = []
        for e in range(E):
            pieces += [own_i[e // 2][e % 2 * TI : (e % 2 + 1) * TI], spare]
        blocks = (
            dot(left_q, right[...], ((0,), (0,))),
            dot(right_q, left[...], ((0,), (0,))),
            jnp.concatenate(pieces * HELD, axis=0).T,
        )
        for kind, block in enumerate(blocks):
            own = own_rows(block)
            for e in range(E):
                ordered[kind, residue_rows(E * q + e), :] = own[PAD * e : PAD * e + TI]
    parts = swap_blocks(
        [
            jnp.concatenate(
                [ordered[kind, (8 * t + i) * R : (8 * t + i + 1) * R] for kind in range(3) for t in range(3)],
                axis=0,
            )
            for i in range(8)
        ]
    )
    for held in range(HELD):
        for e in range(E):
            part = parts[held * E + e]
            for n, slab in enumerate(pack_slabs([part[n * R : (n + 1) * R] for n in range(9)])):
                slots[n, from_owner(held, e), :] = slab
    send[...] = as_messages(all_slots(slots))


def norm_tri(slabs, kind, mask):
    tri = jnp.where(mask, get_kind(slabs, kind), 0.0)
    centered = tri - jnp.mean(tri, axis=0, keepdims=True)
    inv_out = lax.rsqrt(jnp.mean(centered * centered, axis=0, keepdims=True) + norm_eps)
    return centered * inv_out, inv_out


def norm_back(grad, tri_hat, inv_out, mask):
    first_mean = jnp.mean(grad, axis=0, keepdims=True)
    second_mean = jnp.mean(grad * tri_hat, axis=0, keepdims=True)
    return jnp.where(mask, inv_out * (grad - first_mean - tri_hat * second_mean), 0.0)


def output_kernel(
    received, projected, inside, vectors, grad, cotangent, weights, update_hbm, d_outpre, send,
    padded, update, written,
):
    mask = inside[:1, :] > 0
    slabs = unpack_slabs(from_messages(received), 9)
    tri_hat, inv_out = norm_tri(slabs, 0, mask)
    normed_out = (tri_hat * as_column(vectors[8:9]) + as_column(vectors[16:17])).astype(bf16)
    gated_value = dot(weights[...].T, normed_out, ((1,), (0,)))
    gate = jax.nn.sigmoid(projected[4 * C :])
    update[...] = unpadded_rows((gate * gated_value).T, padded)
    write = pltpu.make_async_copy(update, update_hbm, written)
    write.start()
    d_tri = norm_back(grad[...], tri_hat, inv_out, mask)
    mirror_hat, mirror_inv = norm_tri(slabs, 1, mask)
    mirror_grad = jnp.where(mask, get_kind(slabs, 2), 0.0)
    d_mirror = norm_back(mirror_grad, mirror_hat, mirror_inv, mask)
    send[...] = as_messages(pack_slabs(slabs_of(d_tri) + slabs_of(d_mirror)))
    upstream = padded_rows(cotangent[...], padded).T
    d_outpre[...] = (upstream * gated_value * gate * (1.0 - gate)).astype(bf16)
    write.wait()


def padded_columns(rows):
    spare = jnp.zeros((PAD - TI, 128), f32)
    pieces = []
    for e in range(E):
        pieces += [rows[TI * e : TI * (e + 1)], spare]
    block = jnp.concatenate(pieces, axis=0)
    own = own_block((WIDTH, 128))
    return jnp.concatenate(
        [jnp.where(own == held, block, 0.0) for held in range(HELD)], axis=0
    ).astype(bf16)


def back_kernel(received, left_all, right_all, send, slots, ordered):
    fill_slots(slots, received)
    parts = swap_blocks(parts_of(slots, 2))
    for kind in range(2):
        for t in range(3):
            for i in range(8):
                n = 3 * kind + t
                ordered[kind, pl.ds((8 * t + i) * R, R), :] = parts[i][n * R : (n + 1) * R]
    d_left = jnp.zeros((FOLD, 128), f32)
    d_right = jnp.zeros((FOLD, 128), f32)
    for q in range(Q):
        by_i, by_j = (
            padded_columns(
                jnp.concatenate([ordered[kind, residue_rows(E * q + e), :] for e in range(E)], axis=0)
            )
            for kind in range(2)
        )
        d_right = d_right + dot(left_all[q], by_i, ((1,), (0,)))
        d_left = d_left + dot(right_all[q], by_j, ((1,), (0,)))
    sides = (d_left, d_right)
    parts = swap_blocks(
        [
            jnp.concatenate(
                [
                    sides[side][(8 * t + k) * RF : (8 * t + k + 1) * RF]
                    for side in range(2)
                    for t in range(3)
                ],
                axis=0,
            )
            for k in range(8)
        ]
    )
    for held in range(HELD):
        for e in range(E):
            part = parts[held * E + e]
            for n, slab in enumerate(pack_slabs([part[n * RF : (n + 1) * RF] for n in range(6)])):
                for half in range(2):
                    start = HELD * (R * e + RF * half) + held
                    slots[n, pl.ds(start, RF, stride=HELD), :] = slab
    send[...] = as_messages(all_slots(slots))


def input_kernel(
    received, projected, inside, vectors, d_outpre, pair, weights, pair_grad, padded
):
    slabs = unpack_slabs(from_messages(received), 6)
    mask = inside[:1, :]
    d_left = get_kind(slabs, 0) * mask
    d_right = get_kind(slabs, 1) * mask
    left_val, right_val = projected[:C], projected[C : 2 * C]
    left_sig = jax.nn.sigmoid(projected[2 * C : 3 * C])
    right_sig = jax.nn.sigmoid(projected[3 * C : 4 * C])
    d_proj = jnp.concatenate(
        [
            (d_left * left_sig).astype(bf16),
            (d_right * right_sig).astype(bf16),
            (d_left * left_val * left_sig * (1.0 - left_sig)).astype(bf16),
            (d_right * right_val * right_sig * (1.0 - right_sig)).astype(bf16),
            d_outpre[...],
        ],
        axis=0,
    )
    grad = dot(weights[...], d_proj, ((1,), (0,))).T * vectors[:1]
    hat, inv_in = norm_rows(padded_rows(pair[...], padded))
    first_mean = jnp.mean(grad, axis=1, keepdims=True)
    second_mean = jnp.mean(grad * hat, axis=1, keepdims=True)
    pair_grad[...] = unpadded_rows(inv_in * (grad - first_mean - hat * second_mean), padded)


def call(kernel, outs, scratch, *operands, inputs=None, written=(), vmem=40):
    inputs = inputs or [pltpu.VMEM] * len(operands)
    return pl.pallas_call(
        kernel,
        out_shape=[jax.ShapeDtypeStruct(shape, dtype) for shape, dtype in outs],
        in_specs=[pl.BlockSpec(memory_space=space) for space in inputs],
        out_specs=[
            pl.BlockSpec(memory_space=pl.ANY if n in written else pltpu.VMEM)
            for n in range(len(outs))
        ],
        scratch_shapes=[
            pltpu.VMEM(shape, f32) if isinstance(shape, tuple) else shape for shape in scratch
        ],
        compiler_params=pltpu.CompilerParams(vmem_limit_bytes=vmem * 1024 * 1024),
        name=kernel.__name__,
    )(*operands)


def exchange(messages):
    return lax.all_to_all(messages, OWNERS, 0, 0, tiled=True)


def body(pair, crop, in_gain, in_bias, in_weights, out_gain, out_bias, out_weights, cotangent):
    padded = (LANES, C)
    tile = ((TI, TK, C), bf16)
    pair = pair.transpose(1, 0, 2)
    cotangent = cotangent.transpose(1, 0, 2)
    in_gain, in_bias, out_gain, out_bias = (
        v.reshape(1, C) for v in (in_gain, in_bias, out_gain, out_bias)
    )
    def messages(kinds):
        return ((C // HELD, HELD, 128 * packed_count(kinds)), bf16)

    def slots(kinds):
        return (packed_count(kinds), C, 128)

    every_block = ((Q, FOLD, 128), bf16)
    own = ((FOLD, 128), bf16)
    send, projected, inside, vectors, grad = call(
        project_kernel,
        [messages(3), ((5 * C, LANES), f32), ((8, LANES), f32), ((24, C), f32), ((C, LANES), f32)],
        [
            padded, (5 * C, LANES), pltpu.SMEM((N,), jnp.int32),
            pltpu.VMEM((TI, TK, C), bf16), (1, C), (1, C), pltpu.VMEM((C, 5 * C), bf16),
            (1, C), (1, C), pltpu.VMEM((TI, TK, C), bf16), pltpu.VMEM((C, C), bf16),
            pltpu.SemaphoreType.DMA((10,)),
        ],
        crop, pair, in_gain, in_bias, in_weights, out_gain, out_bias, cotangent, out_weights,
        inputs=[pl.ANY] * 9,
        written=(1,),
        vmem=58,
    )
    gathered, left, right = call(
        collect_kernel,
        [((3 * PACK, 128), bf16), own, own],
        [slots(3)],
        exchange(send),
    )
    left_all, right_all, send = call(
        triangle_kernel,
        [every_block, every_block, messages(3)],
        [slots(3), (3, N, 128), (FOLD, 128)],
        lax.all_gather(gathered, "zhi", axis=0), left, right,
    )
    update, d_outpre, send = call(
        output_kernel,
        [tile, ((C, LANES), bf16), messages(2)],
        [
            padded, pltpu.VMEM((TI, TK, C), bf16), pltpu.SemaphoreType.DMA(()),
        ],
        exchange(send), projected, inside, vectors, grad, cotangent, out_weights,
        written=(0,),
    )
    (send,) = call(
        back_kernel,
        [messages(2)],
        [slots(2), (2, N, 128)],
        exchange(send), left_all, right_all,
    )
    (pair_grad,) = call(
        input_kernel,
        [tile],
        [padded],
        exchange(send), projected, inside, vectors, d_outpre, pair, in_weights,
    )
    return update.transpose(1, 0, 2), pair_grad.transpose(1, 0, 2)


def solution(mesh):
    split = Mesh(mesh.devices.reshape(2, 4, 2, Q, 16 // Q, 2), ROWS + COLS)
    tiles = P(ROWS, COLS, None)
    in_specs = (tiles, P(), P(), P(), P(), P(), P(), P(), tiles)
    return jax.shard_map(
        body, mesh=split, in_specs=in_specs, out_specs=(tiles, tiles), check_vma=False
    )
```

```python
import jax
import jax.numpy as jnp
from jax import lax
from jax.experimental import pallas as pl
from jax.experimental.pallas import tpu as pltpu
from jax.sharding import Mesh, PartitionSpec as P

norm_eps = 1e-05
f32 = jnp.float32
bf16 = jnp.bfloat16
ROWS = ("xlo", "y", "core")
COLS = ("zhi", "zlo", "xhi")
OWNERS = ("zlo", "xhi", "xlo", "y", "core")
TK, TI, PAD = 24, 12, 16
LANES = TK * PAD
E, R, Q = 4, 16, 8
HELD = 8 // E
WIDTH = 128 // HELD
C = 128
N = 384
FOLD = N // 2
PACK = FOLD * TI // PAD
GROUP = FOLD - PACK
RF = R // 2


def dot(first_op, second_op, dims):
    return lax.dot_general(first_op, second_op, (dims, ((), ())), preferred_element_type=f32)


def swap_blocks(parts):
    parts = list(parts)
    block = lax.broadcasted_iota(jnp.int32, parts[0].shape, 1) // PAD
    for step in (4, 2, 1):
        upper = (block & step) != 0
        for a in range(8):
            if a & step:
                continue
            b = a | step
            low, high = parts[a], parts[b]
            parts[a] = jnp.where(upper, pltpu.roll(high, step * PAD, 1), low)
            parts[b] = jnp.where(upper, high, pltpu.roll(low, 128 - step * PAD, 1))
    return parts


def as_column(row):
    return jnp.broadcast_to(row, (C, C)).T[:, :1]


def padded_rows(tile, scratch):
    tile = tile.astype(f32)
    for i in range(PAD):
        part = tile[i] if i < TI else jnp.zeros((TK, C), f32)
        scratch[pl.ds(i, TK, stride=PAD), :] = part
    return scratch[...]


def unpadded_rows(values, scratch):
    scratch[...] = values
    return jnp.stack([scratch[pl.ds(i, TK, stride=PAD), :] for i in range(TI)]).astype(bf16)


def parts_of(slots):
    return [
        jnp.concatenate([slots[n, from_owner(held, e), :] for n in range(slots.shape[0])], axis=0)
        for held in range(HELD)
        for e in range(E)
    ]


def unpacked_rows(rows, kinds):
    slabs = [rows[n : n + R] for n in range(0, rows.shape[0], R)]
    return unpack_slabs(slabs, 3 * kinds)


def pack_rows(values):
    spare = lax.broadcasted_iota(jnp.int32, (PACK, 128), 1) % PAD >= TI
    last = values[PACK:]
    moved = [pltpu.roll(last, TI - (PAD - TI) * g, 1) for g in range(3)]
    return jnp.where(spare, jnp.concatenate(moved, axis=0), values[:PACK])


def unpack_rows(packed):
    lane = lax.broadcasted_iota(jnp.int32, (GROUP, 128), 1) % PAD
    last = jnp.zeros((GROUP, 128), f32)
    for g in range(3):
        back = pltpu.roll(packed[GROUP * g : GROUP * (g + 1)], 128 - TI + (PAD - TI) * g, 1)
        last = jnp.where(lane // (PAD - TI) == g, back, last)
    spare = lax.broadcasted_iota(jnp.int32, (PACK, 128), 1) % PAD >= TI
    return jnp.concatenate([jnp.where(spare, 0.0, packed), last], axis=0)


def own_block(shape):
    return lax.broadcasted_iota(jnp.int32, shape, 1) // WIDTH


def norm_rows(values):
    centered = values - jnp.mean(values, axis=1, keepdims=True)
    inv_std = lax.rsqrt(jnp.mean(centered * centered, axis=1, keepdims=True) + norm_eps)
    return centered * inv_std, inv_std


def slabs_of(values):
    return [values[:, 128 * t : 128 * (t + 1)] for t in range(3)]


def get_kind(slabs, kind):
    return jnp.concatenate(slabs[3 * kind : 3 * kind + 3], axis=1)


def pack_slabs(slabs):
    rest, packed = list(slabs), []
    lane = lax.broadcasted_iota(jnp.int32, rest[0].shape, 1) % PAD
    while len(rest) >= 4:
        for g in range(3):
            moved = pltpu.roll(rest[3], TI - (PAD - TI) * g, 1)
            packed.append(jnp.where(lane >= TI, moved, rest[g]))
        rest = rest[4:]
    return packed + rest


def unpack_slabs(packed, count):
    rest, slabs = list(packed), []
    lane = lax.broadcasted_iota(jnp.int32, rest[0].shape, 1) % PAD
    while count - len(slabs) >= 4:
        back = [pltpu.roll(rest[g], 128 - TI + (PAD - TI) * g, 1) for g in range(3)]
        last = jnp.where(lane < 4, back[0], jnp.where(lane < 8, back[1], back[2]))
        slabs += rest[:3] + [last]
        rest = rest[3:]
    return slabs + rest


def packed_count(kinds):
    return 3 * kinds - 3 * kinds // 4


def as_messages(packed):
    return jnp.concatenate(packed, axis=1).reshape(C // HELD, HELD, -1).astype(bf16)


def from_messages(received):
    rows = received[...].astype(f32).reshape(C, -1)
    return [rows[:, n : n + 128] for n in range(0, rows.shape[1], 128)]


def fill_slots(slots, received):
    for n, slab in enumerate(from_messages(received)):
        slots[n, :, :] = slab


def all_slots(slots):
    return [slots[n, :, :] for n in range(slots.shape[0])]


def from_owner(held, e):
    return pl.ds(HELD * R * e + held, R, stride=HELD)


def project_kernel(
    crop_hbm, pair_hbm, gain_hbm, bias_hbm, weights_hbm, out_gain_hbm, out_bias_hbm,
    cotangent_hbm, out_weights_hbm, send, projected, inside, vectors, grad,
    padded, crop, pair, gain, bias, weights, out_gain, out_bias,
    cotangent, out_weights, arrived,
):
    sources = (
        crop_hbm, pair_hbm, gain_hbm, bias_hbm, weights_hbm, out_gain_hbm, out_bias_hbm,
        cotangent_hbm, out_weights_hbm,
    )
    targets = (crop, pair, gain, bias, weights, out_gain, out_bias, cotangent, out_weights)
    loads = [
        pltpu.make_async_copy(source, target, arrived.at[n])
        for n, (source, target) in enumerate(zip(sources, targets))
    ]
    for load in loads:
        load.start()
    loads[1].wait()
    hat, _ = norm_rows(padded_rows(pair[...], padded))
    loads[2].wait()
    loads[3].wait()
    normed = (hat * gain[...] + bias[...]).astype(bf16)
    loads[4].wait()
    projected[...] = dot(weights[...].T, normed, ((1,), (1,)))

    loads[0].wait()
    row_pos = lax.axis_index(ROWS)
    col_pos = lax.axis_index(COLS)
    lane = lax.broadcasted_iota(jnp.int32, (8, LANES), 1)
    crop_rows = jnp.zeros((8, LANES), jnp.int32)
    crop_cols = jnp.full((8, LANES), -1, jnp.int32)
    for k in range(TK):
        crop_rows = jnp.where(lane // PAD == k, crop[row_pos * TK + k], crop_rows)
    for i in range(TI):
        crop_cols = jnp.where(lane % PAD == i, crop[col_pos * TI + i], crop_cols)
    same = (crop_rows == crop_cols).astype(f32)
    inside[...] = same
    mask = same[:1, :]
    left = mask * jax.nn.sigmoid(projected[2 * C : 3 * C]) * projected[:C]
    right = mask * jax.nn.sigmoid(projected[3 * C : 4 * C]) * projected[C : 2 * C]
    for load in loads[5:]:
        load.wait()
    upstream = padded_rows(cotangent[...], padded).T
    d_value = (upstream * jax.nn.sigmoid(projected[4 * C :])).astype(bf16)
    value_grad = dot(out_weights[...], d_value, ((1,), (0,))) * as_column(out_gain[...])
    grad[...] = value_grad
    masked_grad = jnp.where(mask > 0, value_grad, 0.0)
    send[...] = as_messages(
        pack_slabs(slabs_of(left) + slabs_of(right) + slabs_of(masked_grad))
    )
    vectors[...] = jnp.concatenate(
        [jnp.broadcast_to(v[...], (8, C)) for v in (gain, out_gain, out_bias)], axis=0
    )


def collect_kernel(received, gathered, left, right, slots):
    fill_slots(slots, received)
    parts = [unpacked_rows(part, 3) for part in swap_blocks(parts_of(slots))]
    for kind in range(3):
        pieces = []
        for t in range(3):
            for k in range(8):
                slab = parts[k][3 * kind + t]
                pieces.append(slab[:RF] + slab[RF:])
        whole = jnp.concatenate(pieces, axis=0)
        gathered[PACK * kind : PACK * (kind + 1)] = pack_rows(whole).astype(bf16)
        if kind < 2:
            (left, right)[kind][...] = whole.astype(bf16)


def residue_rows(column):
    return pl.ds(column % 2 * TI * R + column // 2, TI, stride=R)


def own_rows(block):
    lanes = own_block((WIDTH, 128))
    own = block[:WIDTH]
    for held in range(1, HELD):
        own = jnp.where(lanes == held, block[WIDTH * held : WIDTH * (held + 1)], own)
    return own


def triangle_kernel(gathered, left, right, left_all, right_all, send, slots, ordered, folded):
    place = 2 * (lax.axis_index("zhi") % (Q // 2))
    spare = jnp.zeros((PAD - TI, 128), f32)
    for q in range(Q):
        left_q = unpack_rows(gathered[q, :PACK].astype(f32)).astype(bf16)
        right_q = unpack_rows(gathered[q, PACK : 2 * PACK].astype(f32)).astype(bf16)
        left_all[q] = left_q
        right_all[q] = right_q
        folded[...] = unpack_rows(gathered[q, 2 * PACK :].astype(f32))
        own_i = [folded[pl.ds(place + half, TK, stride=RF), :] for half in range(2)]
        pieces = []
        for e in range(E):
            pieces += [own_i[e // 2][e % 2 * TI : (e % 2 + 1) * TI], spare]
        blocks = (
            dot(left_q, right[...], ((0,), (0,))),
            dot(right_q, left[...], ((0,), (0,))),
            jnp.concatenate(pieces * HELD, axis=0).T,
        )
        for kind, block in enumerate(blocks):
            own = own_rows(block)
            for e in range(E):
                ordered[kind, residue_rows(E * q + e), :] = own[PAD * e : PAD * e + TI]
    parts = swap_blocks(
        [
            jnp.concatenate(
                pack_slabs(
                    [
                        ordered[kind, (8 * t + i) * R : (8 * t + i + 1) * R]
                        for kind in range(3)
                        for t in range(3)
                    ]
                ),
                axis=0,
            )
            for i in range(8)
        ]
    )
    for held in range(HELD):
        for e in range(E):
            part = parts[held * E + e]
            for n in range(slots.shape[0]):
                slots[n, from_owner(held, e), :] = part[n * R : (n + 1) * R]
    send[...] = as_messages(all_slots(slots))


def norm_tri(slabs, kind, mask):
    tri = jnp.where(mask, get_kind(slabs, kind), 0.0)
    centered = tri - jnp.mean(tri, axis=0, keepdims=True)
    inv_out = lax.rsqrt(jnp.mean(centered * centered, axis=0, keepdims=True) + norm_eps)
    return centered * inv_out, inv_out


def norm_back(grad, tri_hat, inv_out, mask):
    first_mean = jnp.mean(grad, axis=0, keepdims=True)
    second_mean = jnp.mean(grad * tri_hat, axis=0, keepdims=True)
    return jnp.where(mask, inv_out * (grad - first_mean - tri_hat * second_mean), 0.0)


def output_kernel(
    received, projected, inside, vectors, grad, cotangent, weights, update_hbm, d_outpre, send,
    padded, update, written,
):
    mask = inside[:1, :] > 0
    slabs = unpack_slabs(from_messages(received), 9)
    tri_hat, inv_out = norm_tri(slabs, 0, mask)
    normed_out = (tri_hat * as_column(vectors[8:9]) + as_column(vectors[16:17])).astype(bf16)
    gated_value = dot(weights[...].T, normed_out, ((1,), (0,)))
    gate = jax.nn.sigmoid(projected[4 * C :])
    update[...] = unpadded_rows((gate * gated_value).T, padded)
    write = pltpu.make_async_copy(update, update_hbm, written)
    write.start()
    d_tri = norm_back(grad[...], tri_hat, inv_out, mask)
    mirror_hat, mirror_inv = norm_tri(slabs, 1, mask)
    mirror_grad = jnp.where(mask, get_kind(slabs, 2), 0.0)
    d_mirror = norm_back(mirror_grad, mirror_hat, mirror_inv, mask)
    send[...] = as_messages(pack_slabs(slabs_of(d_tri) + slabs_of(d_mirror)))
    upstream = padded_rows(cotangent[...], padded).T
    d_outpre[...] = (upstream * gated_value * gate * (1.0 - gate)).astype(bf16)
    write.wait()


def padded_columns(rows):
    spare = jnp.zeros((PAD - TI, 128), f32)
    pieces = []
    for e in range(E):
        pieces += [rows[TI * e : TI * (e + 1)], spare]
    block = jnp.concatenate(pieces, axis=0)
    own = own_block((WIDTH, 128))
    return jnp.concatenate(
        [jnp.where(own == held, block, 0.0) for held in range(HELD)], axis=0
    ).astype(bf16)


def back_kernel(received, left_all, right_all, send, slots, ordered):
    fill_slots(slots, received)
    parts = [unpacked_rows(part, 2) for part in swap_blocks(parts_of(slots))]
    for kind in range(2):
        for t in range(3):
            for i in range(8):
                ordered[kind, pl.ds((8 * t + i) * R, R), :] = parts[i][3 * kind + t]
    d_left = jnp.zeros((FOLD, 128), f32)
    d_right = jnp.zeros((FOLD, 128), f32)
    for q in range(Q):
        by_i, by_j = (
            padded_columns(
                jnp.concatenate([ordered[kind, residue_rows(E * q + e), :] for e in range(E)], axis=0)
            )
            for kind in range(2)
        )
        d_right = d_right + dot(left_all[q], by_i, ((1,), (0,)))
        d_left = d_left + dot(right_all[q], by_j, ((1,), (0,)))
    sides = (d_left, d_right)
    parts = swap_blocks(
        [
            jnp.concatenate(
                pack_slabs(
                    [
                        sides[side][(8 * t + k) * RF : (8 * t + k + 1) * RF]
                        for side in range(2)
                        for t in range(3)
                    ]
                ),
                axis=0,
            )
            for k in range(8)
        ]
    )
    for held in range(HELD):
        for e in range(E):
            part = parts[held * E + e]
            for n in range(slots.shape[0]):
                for half in range(2):
                    start = HELD * (R * e + RF * half) + held
                    slots[n, pl.ds(start, RF, stride=HELD), :] = part[n * RF : (n + 1) * RF]
    send[...] = as_messages(all_slots(slots))


def input_kernel(
    received, projected, inside, vectors, d_outpre, pair, weights, pair_grad, padded
):
    slabs = unpack_slabs(from_messages(received), 6)
    mask = inside[:1, :]
    d_left = get_kind(slabs, 0) * mask
    d_right = get_kind(slabs, 1) * mask
    left_val, right_val = projected[:C], projected[C : 2 * C]
    left_sig = jax.nn.sigmoid(projected[2 * C : 3 * C])
    right_sig = jax.nn.sigmoid(projected[3 * C : 4 * C])
    d_proj = jnp.concatenate(
        [
            (d_left * left_sig).astype(bf16),
            (d_right * right_sig).astype(bf16),
            (d_left * left_val * left_sig * (1.0 - left_sig)).astype(bf16),
            (d_right * right_val * right_sig * (1.0 - right_sig)).astype(bf16),
            d_outpre[...],
        ],
        axis=0,
    )
    grad = dot(weights[...], d_proj, ((1,), (0,))).T * vectors[:1]
    hat, inv_in = norm_rows(padded_rows(pair[...], padded))
    first_mean = jnp.mean(grad, axis=1, keepdims=True)
    second_mean = jnp.mean(grad * hat, axis=1, keepdims=True)
    pair_grad[...] = unpadded_rows(inv_in * (grad - first_mean - hat * second_mean), padded)


def call(kernel, outs, scratch, *operands, inputs=None, written=()):
    inputs = inputs or [pltpu.VMEM] * len(operands)
    return pl.pallas_call(
        kernel,
        out_shape=[jax.ShapeDtypeStruct(shape, dtype) for shape, dtype in outs],
        in_specs=[pl.BlockSpec(memory_space=space) for space in inputs],
        out_specs=[
            pl.BlockSpec(memory_space=pl.ANY if n in written else pltpu.VMEM)
            for n in range(len(outs))
        ],
        scratch_shapes=[
            pltpu.VMEM(shape, f32) if isinstance(shape, tuple) else shape for shape in scratch
        ],
        compiler_params=pltpu.CompilerParams(vmem_limit_bytes=40 * 1024 * 1024),
        name=kernel.__name__,
    )(*operands)


def exchange(messages):
    return lax.all_to_all(messages, OWNERS, 0, 0, tiled=True)


def body(pair, crop, in_gain, in_bias, in_weights, out_gain, out_bias, out_weights, cotangent):
    padded = (LANES, C)
    tile = ((TI, TK, C), bf16)
    pair = pair.transpose(1, 0, 2)
    cotangent = cotangent.transpose(1, 0, 2)
    in_gain, in_bias, out_gain, out_bias = (
        v.reshape(1, C) for v in (in_gain, in_bias, out_gain, out_bias)
    )
    def messages(kinds):
        return ((C // HELD, HELD, 128 * packed_count(kinds)), bf16)

    def slots(kinds):
        return (packed_count(kinds), C, 128)

    every_block = ((Q, FOLD, 128), bf16)
    own = ((FOLD, 128), bf16)
    send, projected, inside, vectors, grad = call(
        project_kernel,
        [messages(3), ((5 * C, LANES), f32), ((8, LANES), f32), ((24, C), f32), ((C, LANES), f32)],
        [
            padded, pltpu.SMEM((N,), jnp.int32),
            pltpu.VMEM((TI, TK, C), bf16), (1, C), (1, C), pltpu.VMEM((C, 5 * C), bf16),
            (1, C), (1, C), pltpu.VMEM((TI, TK, C), bf16), pltpu.VMEM((C, C), bf16),
            pltpu.SemaphoreType.DMA((9,)),
        ],
        *(
            pltpu.with_memory_space_constraint(v, pltpu.HBM)
            for v in (
                crop, pair, in_gain, in_bias, in_weights, out_gain, out_bias, cotangent, out_weights
            )
        ),
        inputs=[pl.ANY] * 9,
    )
    gathered, left, right = call(
        collect_kernel,
        [((3 * PACK, 128), bf16), own, own],
        [slots(3)],
        exchange(send),
    )
    left_all, right_all, send = call(
        triangle_kernel,
        [every_block, every_block, messages(3)],
        [slots(3), (3, N, 128), (FOLD, 128)],
        lax.all_gather(gathered, "zhi", axis=0), left, right,
    )
    update, d_outpre, send = call(
        output_kernel,
        [tile, ((C, LANES), bf16), messages(2)],
        [
            padded, pltpu.VMEM((TI, TK, C), bf16), pltpu.SemaphoreType.DMA(()),
        ],
        exchange(send), projected, inside, vectors, grad, cotangent, out_weights,
        written=(0,),
    )
    (send,) = call(
        back_kernel,
        [messages(2)],
        [slots(2), (2, N, 128)],
        exchange(send), left_all, right_all,
    )
    (pair_grad,) = call(
        input_kernel,
        [tile],
        [padded],
        exchange(send), projected, inside, vectors, d_outpre, pair, in_weights,
    )
    return update.transpose(1, 0, 2), pair_grad.transpose(1, 0, 2)


def solution(mesh):
    split = Mesh(mesh.devices.reshape(2, 4, 2, Q, 16 // Q, 2), ROWS + COLS)
    tiles = P(ROWS, COLS, None)
    in_specs = (tiles, P(), P(), P(), P(), P(), P(), P(), tiles)
    return jax.shard_map(
        body, mesh=split, in_specs=in_specs, out_specs=(tiles, tiles), check_vma=False
    )
```

```python
import jax
import jax.numpy as jnp
from jax import lax
from jax.experimental import pallas as pl
from jax.experimental.pallas import tpu as pltpu
from jax.sharding import Mesh, PartitionSpec as P

norm_eps = 1e-05
f32 = jnp.float32
bf16 = jnp.bfloat16
ROWS = ("xlo", "y", "core")
COLS = ("zhi", "zlo", "xhi")
OWNERS = ("zlo", "xhi", "xlo", "y", "core")
TK, TI, PAD = 24, 12, 16
LANES = TK * PAD
E, R, Q = 4, 16, 8
HELD = 8 // E
WIDTH = 128 // HELD
C = 128
N = 384
FOLD = N // 2
PACK = FOLD * TI // PAD
GROUP = FOLD - PACK
RF = R // 2


def dot(first_op, second_op, dims):
    return lax.dot_general(first_op, second_op, (dims, ((), ())), preferred_element_type=f32)


def swap_blocks(parts):
    parts = list(parts)
    block = lax.broadcasted_iota(jnp.int32, parts[0].shape, 1) // PAD
    for step in (4, 2, 1):
        upper = (block & step) != 0
        for a in range(8):
            if a & step:
                continue
            b = a | step
            low, high = parts[a], parts[b]
            parts[a] = jnp.where(upper, pltpu.roll(high, step * PAD, 1), low)
            parts[b] = jnp.where(upper, high, pltpu.roll(low, 128 - step * PAD, 1))
    return parts


def as_column(row):
    return jnp.broadcast_to(row, (C, C)).T[:, :1]


def padded_rows(tile, scratch):
    tile = tile.astype(f32)
    for i in range(PAD):
        part = tile[i] if i < TI else jnp.zeros((TK, C), f32)
        scratch[pl.ds(i, TK, stride=PAD), :] = part
    return scratch[...]


def unpadded_rows(values, scratch):
    scratch[...] = values
    return jnp.stack([scratch[pl.ds(i, TK, stride=PAD), :] for i in range(TI)]).astype(bf16)


def parts_of(slots):
    return [
        jnp.concatenate([slots[n, from_owner(held, e), :] for n in range(slots.shape[0])], axis=0)
        for held in range(HELD)
        for e in range(E)
    ]


def unpacked_rows(rows, kinds):
    slabs = [rows[n : n + R] for n in range(0, rows.shape[0], R)]
    return unpack_slabs(slabs, 3 * kinds)


def pack_rows(values):
    spare = lax.broadcasted_iota(jnp.int32, (PACK, 128), 1) % PAD >= TI
    last = values[PACK:]
    moved = [pltpu.roll(last, TI - (PAD - TI) * g, 1) for g in range(3)]
    return jnp.where(spare, jnp.concatenate(moved, axis=0), values[:PACK])


def unpack_rows(packed):
    lane = lax.broadcasted_iota(jnp.int32, (GROUP, 128), 1) % PAD
    last = jnp.zeros((GROUP, 128), f32)
    for g in range(3):
        back = pltpu.roll(packed[GROUP * g : GROUP * (g + 1)], 128 - TI + (PAD - TI) * g, 1)
        last = jnp.where(lane // (PAD - TI) == g, back, last)
    spare = lax.broadcasted_iota(jnp.int32, (PACK, 128), 1) % PAD >= TI
    return jnp.concatenate([jnp.where(spare, 0.0, packed), last], axis=0)


def own_block(shape):
    return lax.broadcasted_iota(jnp.int32, shape, 1) // WIDTH


def norm_rows(values):
    centered = values - jnp.mean(values, axis=1, keepdims=True)
    inv_std = lax.rsqrt(jnp.mean(centered * centered, axis=1, keepdims=True) + norm_eps)
    return centered * inv_std, inv_std


def slabs_of(values):
    return [values[:, 128 * t : 128 * (t + 1)] for t in range(3)]


def get_kind(slabs, kind):
    return jnp.concatenate(slabs[3 * kind : 3 * kind + 3], axis=1)


def pack_slabs(slabs):
    rest, packed = list(slabs), []
    lane = lax.broadcasted_iota(jnp.int32, rest[0].shape, 1) % PAD
    while len(rest) >= 4:
        for g in range(3):
            moved = pltpu.roll(rest[3], TI - (PAD - TI) * g, 1)
            packed.append(jnp.where(lane >= TI, moved, rest[g]))
        rest = rest[4:]
    return packed + rest


def unpack_slabs(packed, count):
    rest, slabs = list(packed), []
    lane = lax.broadcasted_iota(jnp.int32, rest[0].shape, 1) % PAD
    while count - len(slabs) >= 4:
        back = [pltpu.roll(rest[g], 128 - TI + (PAD - TI) * g, 1) for g in range(3)]
        last = jnp.where(lane < 4, back[0], jnp.where(lane < 8, back[1], back[2]))
        slabs += rest[:3] + [last]
        rest = rest[3:]
    return slabs + rest


def packed_count(kinds):
    return 3 * kinds - 3 * kinds // 4


def as_messages(packed):
    return jnp.concatenate(packed, axis=1).reshape(C // HELD, HELD, -1).astype(bf16)


def from_messages(received):
    rows = received[...].astype(f32).reshape(C, -1)
    return [rows[:, n : n + 128] for n in range(0, rows.shape[1], 128)]


def fill_slots(slots, received):
    for n, slab in enumerate(from_messages(received)):
        slots[n, :, :] = slab


def all_slots(slots):
    return [slots[n, :, :] for n in range(slots.shape[0])]


def from_owner(held, e):
    return pl.ds(HELD * R * e + held, R, stride=HELD)


def project_kernel(
    crop_hbm, pair_hbm, gain_hbm, bias_hbm, weights_hbm, out_gain_hbm, out_bias_hbm,
    cotangent_hbm, out_weights_hbm, send, projected, inside, vectors, grad, hat, inv_in, upstream,
    padded, crop, pair, gain, bias, weights, out_gain, out_bias,
    cotangent, out_weights, arrived,
):
    sources = (
        crop_hbm, pair_hbm, gain_hbm, bias_hbm, weights_hbm, out_gain_hbm, out_bias_hbm,
        cotangent_hbm, out_weights_hbm,
    )
    targets = (crop, pair, gain, bias, weights, out_gain, out_bias, cotangent, out_weights)
    loads = [
        pltpu.make_async_copy(source, target, arrived.at[n])
        for n, (source, target) in enumerate(zip(sources, targets))
    ]
    for load in loads:
        load.start()
    loads[1].wait()
    pair_hat, scale = norm_rows(padded_rows(pair[...], padded))
    hat[...] = pair_hat
    inv_in[...] = jnp.broadcast_to(scale, (LANES, C))
    loads[2].wait()
    loads[3].wait()
    normed = (pair_hat * gain[...] + bias[...]).astype(bf16)
    loads[4].wait()
    proj = dot(weights[...].T, normed, ((1,), (1,)))
    opened = jax.nn.sigmoid(proj[2 * C :])
    projected[: 2 * C] = proj[: 2 * C]
    projected[2 * C :] = opened

    loads[0].wait()
    row_pos = lax.axis_index(ROWS)
    col_pos = lax.axis_index(COLS)
    lane = lax.broadcasted_iota(jnp.int32, (8, LANES), 1)
    crop_rows = jnp.zeros((8, LANES), jnp.int32)
    crop_cols = jnp.full((8, LANES), -1, jnp.int32)
    for k in range(TK):
        crop_rows = jnp.where(lane // PAD == k, crop[row_pos * TK + k], crop_rows)
    for i in range(TI):
        crop_cols = jnp.where(lane % PAD == i, crop[col_pos * TI + i], crop_cols)
    same = (crop_rows == crop_cols).astype(f32)
    inside[...] = same
    mask = same[:1, :]
    left = mask * opened[:C] * proj[:C]
    right = mask * opened[C : 2 * C] * proj[C : 2 * C]
    for load in loads[5:]:
        load.wait()
    turned = padded_rows(cotangent[...], padded).T
    upstream[...] = turned
    d_value = (turned * opened[2 * C :]).astype(bf16)
    value_grad = dot(out_weights[...], d_value, ((1,), (0,))) * as_column(out_gain[...])
    grad[...] = value_grad
    masked_grad = jnp.where(mask > 0, value_grad, 0.0)
    send[...] = as_messages(
        pack_slabs(slabs_of(left) + slabs_of(right) + slabs_of(masked_grad))
    )
    vectors[...] = jnp.concatenate(
        [jnp.broadcast_to(v[...], (8, C)) for v in (gain, out_gain, out_bias)], axis=0
    )


def collect_kernel(received, gathered, left, right, slots):
    fill_slots(slots, received)
    parts = [unpacked_rows(part, 3) for part in swap_blocks(parts_of(slots))]
    for kind in range(3):
        pieces = []
        for t in range(3):
            for k in range(8):
                slab = parts[k][3 * kind + t]
                pieces.append(slab[:RF] + slab[RF:])
        whole = jnp.concatenate(pieces, axis=0)
        gathered[PACK * kind : PACK * (kind + 1)] = pack_rows(whole).astype(bf16)
        if kind < 2:
            (left, right)[kind][...] = whole.astype(bf16)


def residue_rows(column):
    return pl.ds(column % 2 * TI * R + column // 2, TI, stride=R)


def own_rows(block):
    lanes = own_block((WIDTH, 128))
    own = block[:WIDTH]
    for held in range(1, HELD):
        own = jnp.where(lanes == held, block[WIDTH * held : WIDTH * (held + 1)], own)
    return own


def triangle_kernel(gathered, left, right, left_all, right_all, send, slots, ordered, folded):
    place = 2 * (lax.axis_index("zhi") % (Q // 2))
    spare = jnp.zeros((PAD - TI, 128), f32)
    for q in range(Q):
        lanes = slice(128 * q, 128 * (q + 1))
        left_all[:, lanes] = unpack_rows(gathered[q, :PACK].astype(f32)).astype(bf16)
        right_all[:, lanes] = unpack_rows(gathered[q, PACK : 2 * PACK].astype(f32)).astype(bf16)
    tri = dot(left_all[...], right[...], ((0,), (0,)))
    mirror = dot(right_all[...], left[...], ((0,), (0,)))
    for q in range(Q):
        folded[...] = unpack_rows(gathered[q, 2 * PACK :].astype(f32))
        own_i = [folded[pl.ds(place + half, TK, stride=RF), :] for half in range(2)]
        pieces = []
        for e in range(E):
            pieces += [own_i[e // 2][e % 2 * TI : (e % 2 + 1) * TI], spare]
        blocks = (
            tri[128 * q : 128 * (q + 1)],
            mirror[128 * q : 128 * (q + 1)],
            jnp.concatenate(pieces * HELD, axis=0).T,
        )
        for kind, block in enumerate(blocks):
            own = own_rows(block)
            for e in range(E):
                ordered[kind, residue_rows(E * q + e), :] = own[PAD * e : PAD * e + TI]
    parts = swap_blocks(
        [
            jnp.concatenate(
                pack_slabs(
                    [
                        ordered[kind, (8 * t + i) * R : (8 * t + i + 1) * R]
                        for kind in range(3)
                        for t in range(3)
                    ]
                ),
                axis=0,
            )
            for i in range(8)
        ]
    )
    for held in range(HELD):
        for e in range(E):
            part = parts[held * E + e]
            for n in range(slots.shape[0]):
                slots[n, from_owner(held, e), :] = part[n * R : (n + 1) * R]
    send[...] = as_messages(all_slots(slots))


def norm_tri(slabs, kind, mask):
    tri = jnp.where(mask, get_kind(slabs, kind), 0.0)
    centered = tri - jnp.mean(tri, axis=0, keepdims=True)
    inv_out = lax.rsqrt(jnp.mean(centered * centered, axis=0, keepdims=True) + norm_eps)
    return centered * inv_out, inv_out


def norm_back(grad, tri_hat, inv_out, mask):
    first_mean = jnp.mean(grad, axis=0, keepdims=True)
    second_mean = jnp.mean(grad * tri_hat, axis=0, keepdims=True)
    return jnp.where(mask, inv_out * (grad - first_mean - tri_hat * second_mean), 0.0)


def output_kernel(
    received, projected, inside, vectors, grad, upstream, weights, update_hbm, d_outpre, send,
    padded, update, written,
):
    mask = inside[:1, :] > 0
    slabs = unpack_slabs(from_messages(received), 9)
    tri_hat, inv_out = norm_tri(slabs, 0, mask)
    normed_out = (tri_hat * as_column(vectors[8:9]) + as_column(vectors[16:17])).astype(bf16)
    gated_value = dot(weights[...].T, normed_out, ((1,), (0,)))
    gate = projected[4 * C :]
    update[...] = unpadded_rows((gate * gated_value).T, padded)
    write = pltpu.make_async_copy(update, update_hbm, written)
    write.start()
    d_tri = norm_back(grad[...], tri_hat, inv_out, mask)
    mirror_hat, mirror_inv = norm_tri(slabs, 1, mask)
    mirror_grad = jnp.where(mask, get_kind(slabs, 2), 0.0)
    d_mirror = norm_back(mirror_grad, mirror_hat, mirror_inv, mask)
    send[...] = as_messages(pack_slabs(slabs_of(d_tri) + slabs_of(d_mirror)))
    d_outpre[...] = (upstream[...] * gated_value * gate * (1.0 - gate)).astype(bf16)
    write.wait()


def padded_columns(rows):
    spare = jnp.zeros((PAD - TI, 128), f32)
    pieces = []
    for e in range(E):
        pieces += [rows[TI * e : TI * (e + 1)], spare]
    block = jnp.concatenate(pieces, axis=0)
    own = own_block((WIDTH, 128))
    return jnp.concatenate(
        [jnp.where(own == held, block, 0.0) for held in range(HELD)], axis=0
    ).astype(bf16)


def back_kernel(received, left_all, right_all, send, slots, ordered):
    fill_slots(slots, received)
    parts = [unpacked_rows(part, 2) for part in swap_blocks(parts_of(slots))]
    for kind in range(2):
        for t in range(3):
            for i in range(8):
                ordered[kind, pl.ds((8 * t + i) * R, R), :] = parts[i][3 * kind + t]
    by_i, by_j = (
        jnp.concatenate(
            [
                padded_columns(
                    jnp.concatenate([ordered[kind, residue_rows(E * q + e), :] for e in range(E)], axis=0)
                )
                for q in range(Q)
            ],
            axis=0,
        )
        for kind in range(2)
    )
    d_right = dot(left_all[...], by_i, ((1,), (0,)))
    d_left = dot(right_all[...], by_j, ((1,), (0,)))
    sides = (d_left, d_right)
    parts = swap_blocks(
        [
            jnp.concatenate(
                pack_slabs(
                    [
                        sides[side][(8 * t + k) * RF : (8 * t + k + 1) * RF]
                        for side in range(2)
                        for t in range(3)
                    ]
                ),
                axis=0,
            )
            for k in range(8)
        ]
    )
    for held in range(HELD):
        for e in range(E):
            part = parts[held * E + e]
            for n in range(slots.shape[0]):
                for half in range(2):
                    start = HELD * (R * e + RF * half) + held
                    slots[n, pl.ds(start, RF, stride=HELD), :] = part[n * RF : (n + 1) * RF]
    send[...] = as_messages(all_slots(slots))


def input_kernel(
    received, projected, inside, vectors, d_outpre, hat, inv_in, weights, pair_grad, padded
):
    slabs = unpack_slabs(from_messages(received), 6)
    mask = inside[:1, :]
    d_left = get_kind(slabs, 0) * mask
    d_right = get_kind(slabs, 1) * mask
    left_val, right_val = projected[:C], projected[C : 2 * C]
    left_sig, right_sig = projected[2 * C : 3 * C], projected[3 * C : 4 * C]
    d_proj = jnp.concatenate(
        [
            (d_left * left_sig).astype(bf16),
            (d_right * right_sig).astype(bf16),
            (d_left * left_val * left_sig * (1.0 - left_sig)).astype(bf16),
            (d_right * right_val * right_sig * (1.0 - right_sig)).astype(bf16),
            d_outpre[...],
        ],
        axis=0,
    )
    grad = dot(weights[...], d_proj, ((1,), (0,))).T * vectors[:1]
    first_mean = jnp.mean(grad, axis=1, keepdims=True)
    second_mean = jnp.mean(grad * hat[...], axis=1, keepdims=True)
    pair_grad[...] = unpadded_rows(
        inv_in[...] * (grad - first_mean - hat[...] * second_mean), padded
    )


def call(kernel, outs, scratch, *operands, inputs=None, written=()):
    inputs = inputs or [pltpu.VMEM] * len(operands)
    return pl.pallas_call(
        kernel,
        out_shape=[jax.ShapeDtypeStruct(shape, dtype) for shape, dtype in outs],
        in_specs=[pl.BlockSpec(memory_space=space) for space in inputs],
        out_specs=[
            pl.BlockSpec(memory_space=pl.ANY if n in written else pltpu.VMEM)
            for n in range(len(outs))
        ],
        scratch_shapes=[
            pltpu.VMEM(shape, f32) if isinstance(shape, tuple) else shape for shape in scratch
        ],
        compiler_params=pltpu.CompilerParams(vmem_limit_bytes=40 * 1024 * 1024),
        name=kernel.__name__,
    )(*operands)


def exchange(messages):
    return lax.all_to_all(messages, OWNERS, 0, 0, tiled=True)


def body(pair, crop, in_gain, in_bias, in_weights, out_gain, out_bias, out_weights, cotangent):
    padded = (LANES, C)
    tile = ((TI, TK, C), bf16)
    pair = pair.transpose(1, 0, 2)
    cotangent = cotangent.transpose(1, 0, 2)
    in_gain, in_bias, out_gain, out_bias = (
        v.reshape(1, C) for v in (in_gain, in_bias, out_gain, out_bias)
    )
    def messages(kinds):
        return ((C // HELD, HELD, 128 * packed_count(kinds)), bf16)

    def slots(kinds):
        return (packed_count(kinds), C, 128)

    every_block = ((FOLD, Q * 128), bf16)
    own = ((FOLD, 128), bf16)
    send, projected, inside, vectors, grad, hat, inv_in, upstream = call(
        project_kernel,
        [
            messages(3), ((5 * C, LANES), f32), ((8, LANES), f32), ((24, C), f32), ((C, LANES), f32),
            (padded, f32), (padded, f32), ((C, LANES), f32),
        ],
        [
            padded, pltpu.SMEM((N,), jnp.int32),
            pltpu.VMEM((TI, TK, C), bf16), (1, C), (1, C), pltpu.VMEM((C, 5 * C), bf16),
            (1, C), (1, C), pltpu.VMEM((TI, TK, C), bf16), pltpu.VMEM((C, C), bf16),
            pltpu.SemaphoreType.DMA((9,)),
        ],
        *(
            pltpu.with_memory_space_constraint(v, pltpu.HBM)
            for v in (
                crop, pair, in_gain, in_bias, in_weights, out_gain, out_bias, cotangent, out_weights
            )
        ),
        inputs=[pl.ANY] * 9,
    )
    gathered, left, right = call(
        collect_kernel,
        [((3 * PACK, 128), bf16), own, own],
        [slots(3)],
        exchange(send),
    )
    left_all, right_all, send = call(
        triangle_kernel,
        [every_block, every_block, messages(3)],
        [slots(3), (3, N, 128), (FOLD, 128)],
        lax.all_gather(gathered, "zhi", axis=0), left, right,
    )
    update, d_outpre, send = call(
        output_kernel,
        [tile, ((C, LANES), bf16), messages(2)],
        [
            padded, pltpu.VMEM((TI, TK, C), bf16), pltpu.SemaphoreType.DMA(()),
        ],
        exchange(send), projected, inside, vectors, grad, upstream, out_weights,
        written=(0,),
    )
    (send,) = call(
        back_kernel,
        [messages(2)],
        [slots(2), (2, N, 128)],
        exchange(send), left_all, right_all,
    )
    (pair_grad,) = call(
        input_kernel,
        [tile],
        [padded],
        exchange(send), projected, inside, vectors, d_outpre, hat, inv_in, in_weights,
    )
    return update.transpose(1, 0, 2), pair_grad.transpose(1, 0, 2)


def solution(mesh):
    split = Mesh(mesh.devices.reshape(2, 4, 2, Q, 16 // Q, 2), ROWS + COLS)
    tiles = P(ROWS, COLS, None)
    in_specs = (tiles, P(), P(), P(), P(), P(), P(), P(), tiles)
    return jax.shard_map(
        body, mesh=split, in_specs=in_specs, out_specs=(tiles, tiles), check_vma=False
    )
```

```python
import jax
import jax.numpy as jnp
from jax import lax
from jax.experimental import pallas as pl
from jax.experimental.pallas import tpu as pltpu
from jax.sharding import Mesh, PartitionSpec as P

norm_eps = 1e-05
f32 = jnp.float32
bf16 = jnp.bfloat16
ROWS = ("xlo", "y", "core")
COLS = ("zhi", "zlo", "xhi")
OWNERS = ("zlo", "xhi", "xlo", "y", "core")
TK, TI, PAD = 24, 12, 16
LANES = TK * PAD
E, R, Q = 4, 16, 8
HELD = 8 // E
WIDTH = 128 // HELD
C = 128
N = 384
FOLD = N // 2
SPAN = N + 4 * 16
PACK = FOLD * TI // PAD
GROUP = FOLD - PACK
RF = R // 2


def dot(first_op, second_op, dims):
    return lax.dot_general(first_op, second_op, (dims, ((), ())), preferred_element_type=f32)


def swap_blocks(parts):
    parts = list(parts)
    block = lax.broadcasted_iota(jnp.int32, parts[0].shape, 1) // PAD
    for step in (4, 2, 1):
        upper = (block & step) != 0
        for a in range(8):
            if a & step:
                continue
            b = a | step
            low, high = parts[a], parts[b]
            parts[a] = jnp.where(upper, pltpu.roll(high, step * PAD, 1), low)
            parts[b] = jnp.where(upper, high, pltpu.roll(low, 128 - step * PAD, 1))
    return parts


def as_column(row):
    return jnp.broadcast_to(row, (C, C)).T[:, :1]


def padded_rows(tile, scratch):
    tile = tile.astype(f32)
    for i in range(PAD):
        part = tile[i] if i < TI else jnp.zeros((TK, C), f32)
        scratch[pl.ds(i, TK, stride=PAD), :] = part
    return scratch[...]


def unpadded_rows(values, scratch):
    scratch[...] = values
    return jnp.stack([scratch[pl.ds(i, TK, stride=PAD), :] for i in range(TI)]).astype(bf16)


def parts_of(slots):
    return [
        jnp.concatenate([slots[n, from_owner(held, e), :] for n in range(slots.shape[0])], axis=0)
        for held in range(HELD)
        for e in range(E)
    ]


def unpacked_rows(rows, kinds):
    slabs = [rows[n : n + R] for n in range(0, rows.shape[0], R)]
    return unpack_slabs(slabs, 3 * kinds)


def pack_rows(values):
    spare = lax.broadcasted_iota(jnp.int32, (PACK, 128), 1) % PAD >= TI
    last = values[PACK:]
    moved = [pltpu.roll(last, TI - (PAD - TI) * g, 1) for g in range(3)]
    return jnp.where(spare, jnp.concatenate(moved, axis=0), values[:PACK])


def unpack_rows(packed):
    lane = lax.broadcasted_iota(jnp.int32, (GROUP, 128), 1) % PAD
    last = jnp.zeros((GROUP, 128), f32)
    for g in range(3):
        back = pltpu.roll(packed[GROUP * g : GROUP * (g + 1)], 128 - TI + (PAD - TI) * g, 1)
        last = jnp.where(lane // (PAD - TI) == g, back, last)
    spare = lax.broadcasted_iota(jnp.int32, (PACK, 128), 1) % PAD >= TI
    return jnp.concatenate([jnp.where(spare, 0.0, packed), last], axis=0)


def own_block(shape):
    return lax.broadcasted_iota(jnp.int32, shape, 1) // WIDTH


def norm_rows(values):
    centered = values - jnp.mean(values, axis=1, keepdims=True)
    inv_std = lax.rsqrt(jnp.mean(centered * centered, axis=1, keepdims=True) + norm_eps)
    return centered * inv_std, inv_std


def slabs_of(values):
    return [values[:, 128 * t : 128 * (t + 1)] for t in range(3)]


def get_kind(slabs, kind):
    return jnp.concatenate(slabs[3 * kind : 3 * kind + 3], axis=1)


def pack_slabs(slabs):
    rest, packed = list(slabs), []
    lane = lax.broadcasted_iota(jnp.int32, rest[0].shape, 1) % PAD
    while len(rest) >= 4:
        for g in range(3):
            moved = pltpu.roll(rest[3], TI - (PAD - TI) * g, 1)
            packed.append(jnp.where(lane >= TI, moved, rest[g]))
        rest = rest[4:]
    return packed + rest


def unpack_slabs(packed, count):
    rest, slabs = list(packed), []
    lane = lax.broadcasted_iota(jnp.int32, rest[0].shape, 1) % PAD
    while count - len(slabs) >= 4:
        back = [pltpu.roll(rest[g], 128 - TI + (PAD - TI) * g, 1) for g in range(3)]
        last = jnp.where(lane < 4, back[0], jnp.where(lane < 8, back[1], back[2]))
        slabs += rest[:3] + [last]
        rest = rest[3:]
    return slabs + rest


def packed_count(kinds):
    return 3 * kinds - 3 * kinds // 4


def as_messages(packed):
    return jnp.concatenate(packed, axis=1).reshape(C // HELD, HELD, -1).astype(bf16)


def from_messages(received):
    rows = received[...].astype(f32).reshape(C, -1)
    return [rows[:, n : n + 128] for n in range(0, rows.shape[1], 128)]


def fill_slots(slots, received):
    for n, slab in enumerate(from_messages(received)):
        slots[n, :, :] = slab


def all_slots(slots):
    return [slots[n, :, :] for n in range(slots.shape[0])]


def from_owner(held, e):
    return pl.ds(HELD * R * e + held, R, stride=HELD)


def project_kernel(
    crop_hbm, pair_hbm, gain_hbm, bias_hbm, weights_hbm, out_gain_hbm, out_bias_hbm,
    cotangent_hbm, out_weights_hbm, send, projected, inside, vectors, grad, hat, inv_in, upstream,
    padded, crop, pair, gain, bias, weights, out_gain, out_bias,
    cotangent, out_weights, arrived,
):
    sources = (
        crop_hbm, pair_hbm, gain_hbm, bias_hbm, weights_hbm, out_gain_hbm, out_bias_hbm,
        cotangent_hbm, out_weights_hbm,
    )
    targets = (crop, pair, gain, bias, weights, out_gain, out_bias, cotangent, out_weights)
    loads = [
        pltpu.make_async_copy(source, target, arrived.at[n])
        for n, (source, target) in enumerate(zip(sources, targets))
    ]
    for load in loads:
        load.start()
    loads[1].wait()
    pair_hat, scale = norm_rows(padded_rows(pair[...], padded))
    hat[...] = pair_hat
    inv_in[...] = jnp.broadcast_to(scale, (LANES, C))
    loads[2].wait()
    loads[3].wait()
    normed = (pair_hat * gain[...] + bias[...]).astype(bf16)
    loads[4].wait()
    proj = dot(weights[...].T, normed, ((1,), (1,)))
    opened = jax.nn.sigmoid(proj[2 * C :])
    projected[: 2 * C] = proj[: 2 * C]
    projected[2 * C :] = opened

    loads[0].wait()
    row_pos = lax.axis_index(ROWS)
    col_pos = lax.axis_index(COLS)
    lane = lax.broadcasted_iota(jnp.int32, (8, LANES), 1)
    crop_rows = jnp.zeros((8, LANES), jnp.int32)
    crop_cols = jnp.full((8, LANES), -1, jnp.int32)
    for k in range(TK):
        crop_rows = jnp.where(lane // PAD == k, crop[row_pos * TK + k], crop_rows)
    for i in range(TI):
        crop_cols = jnp.where(lane % PAD == i, crop[col_pos * TI + i], crop_cols)
    same = (crop_rows == crop_cols).astype(f32)
    inside[...] = same
    mask = same[:1, :]
    left = mask * opened[:C] * proj[:C]
    right = mask * opened[C : 2 * C] * proj[C : 2 * C]
    for load in loads[5:]:
        load.wait()
    turned = padded_rows(cotangent[...], padded).T
    upstream[...] = turned
    d_value = (turned * opened[2 * C :]).astype(bf16)
    value_grad = dot(out_weights[...], d_value, ((1,), (0,))) * as_column(out_gain[...])
    grad[...] = value_grad
    masked_grad = jnp.where(mask > 0, value_grad, 0.0)
    send[...] = as_messages(
        pack_slabs(slabs_of(left) + slabs_of(right) + slabs_of(masked_grad))
    )
    vectors[...] = jnp.concatenate(
        [jnp.broadcast_to(v[...], (8, C)) for v in (gain, out_gain, out_bias)], axis=0
    )


def collect_kernel(received, gathered, left, right, slots):
    fill_slots(slots, received)
    parts = [unpacked_rows(part, 3) for part in swap_blocks(parts_of(slots))]
    for kind in range(3):
        pieces = []
        for t in range(3):
            for k in range(8):
                slab = parts[k][3 * kind + t]
                pieces.append(slab[:RF] + slab[RF:])
        whole = jnp.concatenate(pieces, axis=0)
        gathered[PACK * kind : PACK * (kind + 1)] = pack_rows(whole).astype(bf16)
        if kind < 2:
            (left, right)[kind][...] = whole.astype(bf16)


def residue_rows(column):
    return pl.ds(column % 2 * TI * R + column // 2, TI, stride=R)


def own_rows(block):
    lanes = own_block((WIDTH, 128))
    own = block[:WIDTH]
    for held in range(1, HELD):
        own = jnp.where(lanes == held, block[WIDTH * held : WIDTH * (held + 1)], own)
    return own


def triangle_kernel(gathered, left, right, left_all, right_all, send, slots, ordered, folded):
    place = 2 * (lax.axis_index("zhi") % (Q // 2))
    spare = jnp.zeros((PAD - TI, 128), f32)
    for q in range(Q):
        lanes = slice(128 * q, 128 * (q + 1))
        left_all[:, lanes] = unpack_rows(gathered[q, :PACK].astype(f32)).astype(bf16)
        right_all[:, lanes] = unpack_rows(gathered[q, PACK : 2 * PACK].astype(f32)).astype(bf16)
    tri = dot(left_all[...], right[...], ((0,), (0,)))
    mirror = dot(right_all[...], left[...], ((0,), (0,)))
    for q in range(Q):
        folded[...] = unpack_rows(gathered[q, 2 * PACK :].astype(f32))
        own_i = [folded[pl.ds(place + half, TK, stride=RF), :] for half in range(2)]
        pieces = []
        for e in range(E):
            pieces += [own_i[e // 2][e % 2 * TI : (e % 2 + 1) * TI], spare]
        blocks = (
            tri[128 * q : 128 * (q + 1)],
            mirror[128 * q : 128 * (q + 1)],
            jnp.concatenate(pieces * HELD, axis=0).T,
        )
        for kind, block in enumerate(blocks):
            own = own_rows(block)
            for e in range(E):
                ordered[kind, residue_rows(E * q + e), :] = own[PAD * e : PAD * e + TI]
    parts = swap_blocks(
        [
            jnp.concatenate(
                pack_slabs(
                    [
                        ordered[kind, (8 * t + i) * R : (8 * t + i + 1) * R]
                        for kind in range(3)
                        for t in range(3)
                    ]
                ),
                axis=0,
            )
            for i in range(8)
        ]
    )
    for held in range(HELD):
        for e in range(E):
            part = parts[held * E + e]
            for n in range(slots.shape[0]):
                slots[n, from_owner(held, e), :] = part[n * R : (n + 1) * R]
    send[...] = as_messages(all_slots(slots))


def norm_tri(slabs, kind, mask):
    tri = jnp.where(mask, get_kind(slabs, kind), 0.0)
    centered = tri - jnp.mean(tri, axis=0, keepdims=True)
    inv_out = lax.rsqrt(jnp.mean(centered * centered, axis=0, keepdims=True) + norm_eps)
    return centered * inv_out, inv_out


def norm_back(grad, tri_hat, inv_out, mask):
    first_mean = jnp.mean(grad, axis=0, keepdims=True)
    second_mean = jnp.mean(grad * tri_hat, axis=0, keepdims=True)
    return jnp.where(mask, inv_out * (grad - first_mean - tri_hat * second_mean), 0.0)


def output_kernel(
    received, projected, inside, vectors, grad, upstream, weights, update_hbm, d_outpre, send,
    padded, update, written,
):
    mask = inside[:1, :] > 0
    slabs = unpack_slabs(from_messages(received), 9)
    tri_hat, inv_out = norm_tri(slabs, 0, mask)
    normed_out = (tri_hat * as_column(vectors[8:9]) + as_column(vectors[16:17])).astype(bf16)
    gated_value = dot(weights[...].T, normed_out, ((1,), (0,)))
    gate = projected[4 * C :]
    update[...] = unpadded_rows((gate * gated_value).T, padded)
    write = pltpu.make_async_copy(update, update_hbm, written)
    write.start()
    d_tri = norm_back(grad[...], tri_hat, inv_out, mask)
    mirror_hat, mirror_inv = norm_tri(slabs, 1, mask)
    mirror_grad = jnp.where(mask, get_kind(slabs, 2), 0.0)
    d_mirror = norm_back(mirror_grad, mirror_hat, mirror_inv, mask)
    send[...] = as_messages(pack_slabs(slabs_of(d_tri) + slabs_of(d_mirror)))
    d_outpre[...] = (upstream[...] * gated_value * gate * (1.0 - gate)).astype(bf16)
    write.wait()


def padded_columns(rows):
    spare = jnp.zeros((PAD - TI, 128), f32)
    pieces = []
    for e in range(E):
        pieces += [rows[TI * e : TI * (e + 1)], spare]
    block = jnp.concatenate(pieces, axis=0)
    own = own_block((WIDTH, 128))
    return jnp.concatenate(
        [jnp.where(own == held, block, 0.0) for held in range(HELD)], axis=0
    ).astype(bf16)


def back_kernel(received, left_all, right_all, send, slots, ordered):
    fill_slots(slots, received)
    parts = [unpacked_rows(part, 2) for part in swap_blocks(parts_of(slots))]
    for kind in range(2):
        for t in range(3):
            for i in range(8):
                ordered[kind, pl.ds((8 * t + i) * R, R), :] = parts[i][3 * kind + t]
    by_i, by_j = (
        jnp.concatenate(
            [
                padded_columns(
                    jnp.concatenate([ordered[kind, residue_rows(E * q + e), :] for e in range(E)], axis=0)
                )
                for q in range(Q)
            ],
            axis=0,
        )
        for kind in range(2)
    )
    d_right = dot(left_all[...], by_i, ((1,), (0,)))
    d_left = dot(right_all[...], by_j, ((1,), (0,)))
    sides = (d_left, d_right)
    parts = swap_blocks(
        [
            jnp.concatenate(
                pack_slabs(
                    [
                        sides[side][(8 * t + k) * RF : (8 * t + k + 1) * RF]
                        for side in range(2)
                        for t in range(3)
                    ]
                ),
                axis=0,
            )
            for k in range(8)
        ]
    )
    for held in range(HELD):
        for e in range(E):
            part = parts[held * E + e]
            for n in range(slots.shape[0]):
                for half in range(2):
                    start = HELD * (R * e + RF * half) + held
                    slots[n, pl.ds(start, RF, stride=HELD), :] = part[n * RF : (n + 1) * RF]
    send[...] = as_messages(all_slots(slots))


def input_kernel(
    received, projected, inside, vectors, d_outpre, hat, inv_in, weights, pair_grad, padded
):
    slabs = unpack_slabs(from_messages(received), 6)
    mask = inside[:1, :]
    d_left = get_kind(slabs, 0) * mask
    d_right = get_kind(slabs, 1) * mask
    left_val, right_val = projected[:C], projected[C : 2 * C]
    left_sig, right_sig = projected[2 * C : 3 * C], projected[3 * C : 4 * C]
    d_proj = jnp.concatenate(
        [
            (d_left * left_sig).astype(bf16),
            (d_right * right_sig).astype(bf16),
            (d_left * left_val * left_sig * (1.0 - left_sig)).astype(bf16),
            (d_right * right_val * right_sig * (1.0 - right_sig)).astype(bf16),
            d_outpre[...],
        ],
        axis=0,
    )
    grad = dot(weights[...], d_proj, ((1,), (0,))).T * vectors[:1]
    first_mean = jnp.mean(grad, axis=1, keepdims=True)
    second_mean = jnp.mean(grad * hat[...], axis=1, keepdims=True)
    pair_grad[...] = unpadded_rows(
        inv_in[...] * (grad - first_mean - hat[...] * second_mean), padded
    )


def call(kernel, outs, scratch, *operands, inputs=None, written=()):
    inputs = inputs or [pltpu.VMEM] * len(operands)
    return pl.pallas_call(
        kernel,
        out_shape=[jax.ShapeDtypeStruct(shape, dtype) for shape, dtype in outs],
        in_specs=[pl.BlockSpec(memory_space=space) for space in inputs],
        out_specs=[
            pl.BlockSpec(memory_space=pl.ANY if n in written else pltpu.VMEM)
            for n in range(len(outs))
        ],
        scratch_shapes=[
            pltpu.VMEM(shape, f32) if isinstance(shape, tuple) else shape for shape in scratch
        ],
        compiler_params=pltpu.CompilerParams(vmem_limit_bytes=40 * 1024 * 1024),
        name=kernel.__name__,
    )(*operands)


def exchange(messages):
    return lax.all_to_all(messages, OWNERS, 0, 0, tiled=True)


def body(pair, crop, in_gain, in_bias, in_weights, out_gain, out_bias, out_weights, cotangent):
    padded = (LANES, C)
    tile = ((TI, TK, C), bf16)
    pair = pair.transpose(1, 0, 2)
    cotangent = cotangent.transpose(1, 0, 2)
    in_gain, in_bias, out_gain, out_bias = (
        v.reshape(1, C) for v in (in_gain, in_bias, out_gain, out_bias)
    )
    def messages(kinds):
        return ((C // HELD, HELD, 128 * packed_count(kinds)), bf16)

    def slots(kinds):
        return (packed_count(kinds), C, 128)

    every_block = ((FOLD, Q * 128), bf16)
    own = ((FOLD, 128), bf16)
    send, projected, inside, vectors, grad, hat, inv_in, upstream = call(
        project_kernel,
        [
            messages(3), ((5 * C, LANES), f32), ((8, LANES), f32), ((24, C), f32), ((C, LANES), f32),
            (padded, f32), (padded, f32), ((C, LANES), f32),
        ],
        [
            padded, pltpu.SMEM((N,), jnp.int32),
            pltpu.VMEM((TI, TK, C), bf16), (1, C), (1, C), pltpu.VMEM((C, 5 * C), bf16),
            (1, C), (1, C), pltpu.VMEM((TI, TK, C), bf16), pltpu.VMEM((C, C), bf16),
            pltpu.SemaphoreType.DMA((9,)),
        ],
        *(
            pltpu.with_memory_space_constraint(v, pltpu.HBM)
            for v in (
                crop, pair, in_gain, in_bias, in_weights, out_gain, out_bias, cotangent, out_weights
            )
        ),
        inputs=[pl.ANY] * 9,
    )
    gathered, left, right = call(
        collect_kernel,
        [((3 * PACK, 128), bf16), own, own],
        [slots(3)],
        exchange(send),
    )
    left_all, right_all, send = call(
        triangle_kernel,
        [every_block, every_block, messages(3)],
        [slots(3), (3, SPAN, 128), (FOLD, 128)],
        lax.all_gather(gathered, "zhi", axis=0), left, right,
    )
    update, d_outpre, send = call(
        output_kernel,
        [tile, ((C, LANES), bf16), messages(2)],
        [
            padded, pltpu.VMEM((TI, TK, C), bf16), pltpu.SemaphoreType.DMA(()),
        ],
        exchange(send), projected, inside, vectors, grad, upstream, out_weights,
        written=(0,),
    )
    (send,) = call(
        back_kernel,
        [messages(2)],
        [slots(2), (2, SPAN, 128)],
        exchange(send), left_all, right_all,
    )
    (pair_grad,) = call(
        input_kernel,
        [tile],
        [padded],
        exchange(send), projected, inside, vectors, d_outpre, hat, inv_in, in_weights,
    )
    return update.transpose(1, 0, 2), pair_grad.transpose(1, 0, 2)


def solution(mesh):
    split = Mesh(mesh.devices.reshape(2, 4, 2, Q, 16 // Q, 2), ROWS + COLS)
    tiles = P(ROWS, COLS, None)
    in_specs = (tiles, P(), P(), P(), P(), P(), P(), P(), tiles)
    return jax.shard_map(
        body, mesh=split, in_specs=in_specs, out_specs=(tiles, tiles), check_vma=False
    )
```

```python
import jax
import jax.numpy as jnp
from jax import lax
from jax.experimental import pallas as pl
from jax.experimental.pallas import tpu as pltpu
from jax.sharding import Mesh, PartitionSpec as P

norm_eps = 1e-05
f32 = jnp.float32
bf16 = jnp.bfloat16
ROWS = ("xlo", "y", "core")
COLS = ("zhi", "zlo", "xhi")
OWNERS = ("zlo", "xhi", "xlo", "y", "core")
TK, TI, PAD = 24, 12, 16
LANES = TK * PAD
E, R, Q = 4, 16, 8
HELD = 8 // E
WIDTH = 128 // HELD
C = 128
N = 384
FOLD = N // 2
SPAN = N + 4 * 16
PACK = FOLD * TI // PAD
GROUP = FOLD - PACK
RF = R // 2


def dot(first_op, second_op, dims):
    return lax.dot_general(first_op, second_op, (dims, ((), ())), preferred_element_type=f32)


def swap_blocks(parts):
    parts = list(parts)
    block = lax.broadcasted_iota(jnp.int32, parts[0].shape, 1) // PAD
    for step in (4, 2, 1):
        upper = (block & step) != 0
        for a in range(8):
            if a & step:
                continue
            b = a | step
            low, high = parts[a], parts[b]
            if step == 4:
                turned = pltpu.roll(jnp.where(upper, low, high), 64, 1)
                parts[a] = jnp.where(upper, turned, low)
                parts[b] = jnp.where(upper, high, turned)
                continue
            parts[a] = jnp.where(upper, pltpu.roll(high, step * PAD, 1), low)
            parts[b] = jnp.where(upper, high, pltpu.roll(low, 128 - step * PAD, 1))
    return parts


def as_column(row):
    return jnp.broadcast_to(row, (C, C)).T[:, :1]


def padded_rows(tile, scratch):
    tile = tile.astype(f32)
    for i in range(PAD):
        part = tile[i] if i < TI else jnp.zeros((TK, C), f32)
        scratch[pl.ds(i, TK, stride=PAD), :] = part
    return scratch[...]


def unpadded_rows(values, scratch):
    scratch[...] = values
    return jnp.stack([scratch[pl.ds(i, TK, stride=PAD), :] for i in range(TI)]).astype(bf16)


def parts_of(slots):
    return [
        jnp.concatenate([slots[n, from_owner(held, e), :] for n in range(slots.shape[0])], axis=0)
        for held in range(HELD)
        for e in range(E)
    ]


def unpacked_rows(rows, kinds):
    slabs = [rows[n : n + R] for n in range(0, rows.shape[0], R)]
    return unpack_slabs(slabs, 3 * kinds)


def pack_rows(values):
    spare = lax.broadcasted_iota(jnp.int32, (PACK, 128), 1) % PAD >= TI
    last = values[PACK:]
    moved = [pltpu.roll(last, TI - (PAD - TI) * g, 1) for g in range(3)]
    return jnp.where(spare, jnp.concatenate(moved, axis=0), values[:PACK])


def unpack_rows(packed):
    lane = lax.broadcasted_iota(jnp.int32, (GROUP, 128), 1) % PAD
    last = jnp.zeros((GROUP, 128), f32)
    for g in range(3):
        back = pltpu.roll(packed[GROUP * g : GROUP * (g + 1)], 128 - TI + (PAD - TI) * g, 1)
        last = jnp.where(lane // (PAD - TI) == g, back, last)
    spare = lax.broadcasted_iota(jnp.int32, (PACK, 128), 1) % PAD >= TI
    return jnp.concatenate([jnp.where(spare, 0.0, packed), last], axis=0)


def own_block(shape):
    return lax.broadcasted_iota(jnp.int32, shape, 1) // WIDTH


def norm_rows(values):
    centered = values - jnp.mean(values, axis=1, keepdims=True)
    inv_std = lax.rsqrt(jnp.mean(centered * centered, axis=1, keepdims=True) + norm_eps)
    return centered * inv_std, inv_std


def slabs_of(values):
    return [values[:, 128 * t : 128 * (t + 1)] for t in range(3)]


def get_kind(slabs, kind):
    return jnp.concatenate(slabs[3 * kind : 3 * kind + 3], axis=1)


def pack_slabs(slabs):
    rest, packed = list(slabs), []
    lane = lax.broadcasted_iota(jnp.int32, rest[0].shape, 1) % PAD
    while len(rest) >= 4:
        for g in range(3):
            moved = pltpu.roll(rest[3], TI - (PAD - TI) * g, 1)
            packed.append(jnp.where(lane >= TI, moved, rest[g]))
        rest = rest[4:]
    return packed + rest


def unpack_slabs(packed, count):
    rest, slabs = list(packed), []
    lane = lax.broadcasted_iota(jnp.int32, rest[0].shape, 1) % PAD
    while count - len(slabs) >= 4:
        back = [pltpu.roll(rest[g], 128 - TI + (PAD - TI) * g, 1) for g in range(3)]
        last = jnp.where(lane < 4, back[0], jnp.where(lane < 8, back[1], back[2]))
        slabs += rest[:3] + [last]
        rest = rest[3:]
    return slabs + rest


def packed_count(kinds):
    return 3 * kinds - 3 * kinds // 4


def as_messages(packed):
    return jnp.concatenate(packed, axis=1).astype(bf16).reshape(C // HELD, HELD, -1)


def from_messages(received):
    rows = received[...].reshape(C, -1).astype(f32)
    return [rows[:, n : n + 128] for n in range(0, rows.shape[1], 128)]


def fill_slots(slots, received):
    for n, slab in enumerate(from_messages(received)):
        slots[n, :, :] = slab


def all_slots(slots):
    return [slots[n, :, :] for n in range(slots.shape[0])]


def from_owner(held, e):
    return pl.ds(HELD * R * e + held, R, stride=HELD)


def project_kernel(
    crop_hbm, pair_hbm, gain_hbm, bias_hbm, weights_hbm, out_gain_hbm, out_bias_hbm,
    cotangent_hbm, out_weights_hbm, send, projected, inside, vectors, grad, hat, inv_in, upstream,
    padded, crop, pair, gain, bias, weights, out_gain, out_bias,
    cotangent, out_weights, arrived,
):
    sources = (
        crop_hbm, pair_hbm, gain_hbm, bias_hbm, weights_hbm, out_gain_hbm, out_bias_hbm,
        cotangent_hbm, out_weights_hbm,
    )
    targets = (crop, pair, gain, bias, weights, out_gain, out_bias, cotangent, out_weights)
    loads = [
        pltpu.make_async_copy(source, target, arrived.at[n])
        for n, (source, target) in enumerate(zip(sources, targets))
    ]
    for load in loads:
        load.start()
    loads[1].wait()
    pair_hat, scale = norm_rows(padded_rows(pair[...], padded))
    hat[...] = pair_hat
    inv_in[...] = jnp.broadcast_to(scale, (LANES, C))
    loads[2].wait()
    loads[3].wait()
    normed = (pair_hat * gain[...] + bias[...]).astype(bf16)
    loads[4].wait()
    proj = dot(weights[...].T, normed, ((1,), (1,)))
    opened = jax.nn.sigmoid(proj[2 * C :])
    projected[: 2 * C] = proj[: 2 * C]
    projected[2 * C :] = opened

    loads[0].wait()
    row_pos = lax.axis_index(ROWS)
    col_pos = lax.axis_index(COLS)
    lane = lax.broadcasted_iota(jnp.int32, (8, LANES), 1)
    crop_rows = jnp.zeros((8, LANES), jnp.int32)
    crop_cols = jnp.full((8, LANES), -1, jnp.int32)
    for k in range(TK):
        crop_rows = jnp.where(lane // PAD == k, crop[row_pos * TK + k], crop_rows)
    for i in range(TI):
        crop_cols = jnp.where(lane % PAD == i, crop[col_pos * TI + i], crop_cols)
    same = (crop_rows == crop_cols).astype(f32)
    inside[...] = same
    mask = same[:1, :]
    left = mask * opened[:C] * proj[:C]
    right = mask * opened[C : 2 * C] * proj[C : 2 * C]
    for load in loads[5:]:
        load.wait()
    turned = padded_rows(cotangent[...], padded).T
    upstream[...] = turned
    d_value = (turned * opened[2 * C :]).astype(bf16)
    value_grad = dot(out_weights[...], d_value, ((1,), (0,))) * as_column(out_gain[...])
    grad[...] = value_grad
    masked_grad = jnp.where(mask > 0, value_grad, 0.0)
    send[...] = as_messages(
        pack_slabs(slabs_of(left) + slabs_of(right) + slabs_of(masked_grad))
    )
    vectors[...] = jnp.concatenate(
        [jnp.broadcast_to(v[...], (8, C)) for v in (gain, out_gain, out_bias)], axis=0
    )


def collect_kernel(received, gathered, left, right, slots):
    fill_slots(slots, received)
    parts = [unpacked_rows(part, 3) for part in swap_blocks(parts_of(slots))]
    for kind in range(3):
        pieces = []
        for t in range(3):
            for k in range(8):
                slab = parts[k][3 * kind + t]
                pieces.append(slab[:RF] + slab[RF:])
        whole = jnp.concatenate(pieces, axis=0)
        gathered[PACK * kind : PACK * (kind + 1)] = pack_rows(whole).astype(bf16)
        if kind < 2:
            (left, right)[kind][...] = whole.astype(bf16)


def residue_rows(column):
    return pl.ds(column % 2 * TI * R + column // 2, TI, stride=R)


def own_rows(block):
    lanes = own_block((WIDTH, 128))
    own = block[:WIDTH]
    for held in range(1, HELD):
        own = jnp.where(lanes == held, block[WIDTH * held : WIDTH * (held + 1)], own)
    return own


def triangle_kernel(gathered, left, right, left_all, right_all, send, slots, ordered, folded):
    place = 2 * (lax.axis_index("zhi") % (Q // 2))
    spare = jnp.zeros((PAD - TI, 128), f32)
    for q in range(Q):
        lanes = slice(128 * q, 128 * (q + 1))
        left_all[:, lanes] = unpack_rows(gathered[q, :PACK].astype(f32)).astype(bf16)
        right_all[:, lanes] = unpack_rows(gathered[q, PACK : 2 * PACK].astype(f32)).astype(bf16)
    tri = dot(left_all[...], right[...], ((0,), (0,)))
    mirror = dot(right_all[...], left[...], ((0,), (0,)))
    for q in range(Q):
        folded[...] = unpack_rows(gathered[q, 2 * PACK :].astype(f32))
        own_i = [folded[pl.ds(place + half, TK, stride=RF), :] for half in range(2)]
        pieces = []
        for e in range(E):
            pieces += [own_i[e // 2][e % 2 * TI : (e % 2 + 1) * TI], spare]
        blocks = (
            tri[128 * q : 128 * (q + 1)],
            mirror[128 * q : 128 * (q + 1)],
            jnp.concatenate(pieces * HELD, axis=0).T,
        )
        for kind, block in enumerate(blocks):
            own = own_rows(block)
            for e in range(E):
                ordered[kind, residue_rows(E * q + e), :] = own[PAD * e : PAD * e + TI]
    parts = swap_blocks(
        [
            jnp.concatenate(
                pack_slabs(
                    [
                        ordered[kind, (8 * t + i) * R : (8 * t + i + 1) * R]
                        for kind in range(3)
                        for t in range(3)
                    ]
                ),
                axis=0,
            )
            for i in range(8)
        ]
    )
    for held in range(HELD):
        for e in range(E):
            part = parts[held * E + e]
            for n in range(slots.shape[0]):
                slots[n, from_owner(held, e), :] = part[n * R : (n + 1) * R]
    send[...] = as_messages(all_slots(slots))


def norm_tri(slabs, kind, mask):
    tri = jnp.where(mask, get_kind(slabs, kind), 0.0)
    centered = tri - jnp.mean(tri, axis=0, keepdims=True)
    inv_out = lax.rsqrt(jnp.mean(centered * centered, axis=0, keepdims=True) + norm_eps)
    return centered * inv_out, inv_out


def norm_back(grad, tri_hat, inv_out, mask):
    first_mean = jnp.mean(grad, axis=0, keepdims=True)
    second_mean = jnp.mean(grad * tri_hat, axis=0, keepdims=True)
    return jnp.where(mask, inv_out * (grad - first_mean - tri_hat * second_mean), 0.0)


def output_kernel(
    received, projected, inside, vectors, grad, upstream, weights, update_hbm, d_outpre, send,
    padded, update, written,
):
    mask = inside[:1, :] > 0
    slabs = unpack_slabs(from_messages(received), 9)
    tri_hat, inv_out = norm_tri(slabs, 0, mask)
    normed_out = (tri_hat * as_column(vectors[8:9]) + as_column(vectors[16:17])).astype(bf16)
    gated_value = dot(weights[...].T, normed_out, ((1,), (0,)))
    gate = projected[4 * C :]
    update[...] = unpadded_rows((gate * gated_value).T, padded)
    write = pltpu.make_async_copy(update, update_hbm, written)
    write.start()
    d_tri = norm_back(grad[...], tri_hat, inv_out, mask)
    mirror_hat, mirror_inv = norm_tri(slabs, 1, mask)
    mirror_grad = jnp.where(mask, get_kind(slabs, 2), 0.0)
    d_mirror = norm_back(mirror_grad, mirror_hat, mirror_inv, mask)
    send[...] = as_messages(pack_slabs(slabs_of(d_tri) + slabs_of(d_mirror)))
    d_outpre[...] = (upstream[...] * gated_value * gate * (1.0 - gate)).astype(bf16)
    write.wait()


def padded_columns(rows):
    spare = jnp.zeros((PAD - TI, 128), f32)
    pieces = []
    for e in range(E):
        pieces += [rows[TI * e : TI * (e + 1)], spare]
    block = jnp.concatenate(pieces, axis=0)
    own = own_block((WIDTH, 128))
    return jnp.concatenate(
        [jnp.where(own == held, block, 0.0) for held in range(HELD)], axis=0
    ).astype(bf16)


def back_kernel(received, left_all, right_all, send, slots, ordered):
    fill_slots(slots, received)
    parts = [unpacked_rows(part, 2) for part in swap_blocks(parts_of(slots))]
    for kind in range(2):
        for t in range(3):
            for i in range(8):
                ordered[kind, pl.ds((8 * t + i) * R, R), :] = parts[i][3 * kind + t]
    by_i, by_j = (
        jnp.concatenate(
            [
                padded_columns(
                    jnp.concatenate([ordered[kind, residue_rows(E * q + e), :] for e in range(E)], axis=0)
                )
                for q in range(Q)
            ],
            axis=0,
        )
        for kind in range(2)
    )
    d_right = dot(left_all[...], by_i, ((1,), (0,)))
    d_left = dot(right_all[...], by_j, ((1,), (0,)))
    sides = (d_left, d_right)
    parts = swap_blocks(
        [
            jnp.concatenate(
                pack_slabs(
                    [
                        sides[side][(8 * t + k) * RF : (8 * t + k + 1) * RF]
                        for side in range(2)
                        for t in range(3)
                    ]
                ),
                axis=0,
            )
            for k in range(8)
        ]
    )
    for held in range(HELD):
        for e in range(E):
            part = parts[held * E + e]
            for n in range(slots.shape[0]):
                for half in range(2):
                    start = HELD * (R * e + RF * half) + held
                    slots[n, pl.ds(start, RF, stride=HELD), :] = part[n * RF : (n + 1) * RF]
    send[...] = as_messages(all_slots(slots))


def input_kernel(
    received, projected, inside, vectors, d_outpre, hat, inv_in, weights, pair_grad, padded
):
    slabs = unpack_slabs(from_messages(received), 6)
    mask = inside[:1, :]
    d_left = get_kind(slabs, 0) * mask
    d_right = get_kind(slabs, 1) * mask
    left_val, right_val = projected[:C], projected[C : 2 * C]
    left_sig, right_sig = projected[2 * C : 3 * C], projected[3 * C : 4 * C]
    d_proj = jnp.concatenate(
        [
            (d_left * left_sig).astype(bf16),
            (d_right * right_sig).astype(bf16),
            (d_left * left_val * left_sig * (1.0 - left_sig)).astype(bf16),
            (d_right * right_val * right_sig * (1.0 - right_sig)).astype(bf16),
            d_outpre[...],
        ],
        axis=0,
    )
    grad = dot(weights[...], d_proj, ((1,), (0,))).T * vectors[:1]
    first_mean = jnp.mean(grad, axis=1, keepdims=True)
    second_mean = jnp.mean(grad * hat[...], axis=1, keepdims=True)
    pair_grad[...] = unpadded_rows(
        inv_in[...] * (grad - first_mean - hat[...] * second_mean), padded
    )


def call(kernel, outs, scratch, *operands, inputs=None, written=()):
    inputs = inputs or [pltpu.VMEM] * len(operands)
    return pl.pallas_call(
        kernel,
        out_shape=[jax.ShapeDtypeStruct(shape, dtype) for shape, dtype in outs],
        in_specs=[pl.BlockSpec(memory_space=space) for space in inputs],
        out_specs=[
            pl.BlockSpec(memory_space=pl.ANY if n in written else pltpu.VMEM)
            for n in range(len(outs))
        ],
        scratch_shapes=[
            pltpu.VMEM(shape, f32) if isinstance(shape, tuple) else shape for shape in scratch
        ],
        compiler_params=pltpu.CompilerParams(vmem_limit_bytes=40 * 1024 * 1024),
        name=kernel.__name__,
    )(*operands)


def exchange(messages):
    return lax.all_to_all(messages, OWNERS, 0, 0, tiled=True)


def body(pair, crop, in_gain, in_bias, in_weights, out_gain, out_bias, out_weights, cotangent):
    padded = (LANES, C)
    tile = ((TI, TK, C), bf16)
    pair = pair.transpose(1, 0, 2)
    cotangent = cotangent.transpose(1, 0, 2)
    in_gain, in_bias, out_gain, out_bias = (
        v.reshape(1, C) for v in (in_gain, in_bias, out_gain, out_bias)
    )
    def messages(kinds):
        return ((C // HELD, HELD, 128 * packed_count(kinds)), bf16)

    def slots(kinds):
        return (packed_count(kinds), C, 128)

    every_block = ((FOLD, Q * 128), bf16)
    own = ((FOLD, 128), bf16)
    send, projected, inside, vectors, grad, hat, inv_in, upstream = call(
        project_kernel,
        [
            messages(3), ((5 * C, LANES), f32), ((8, LANES), f32), ((24, C), f32), ((C, LANES), f32),
            (padded, f32), (padded, f32), ((C, LANES), f32),
        ],
        [
            padded, pltpu.SMEM((N,), jnp.int32),
            pltpu.VMEM((TI, TK, C), bf16), (1, C), (1, C), pltpu.VMEM((C, 5 * C), bf16),
            (1, C), (1, C), pltpu.VMEM((TI, TK, C), bf16), pltpu.VMEM((C, C), bf16),
            pltpu.SemaphoreType.DMA((9,)),
        ],
        *(
            pltpu.with_memory_space_constraint(v, pltpu.HBM)
            for v in (
                crop, pair, in_gain, in_bias, in_weights, out_gain, out_bias, cotangent, out_weights
            )
        ),
        inputs=[pl.ANY] * 9,
    )
    gathered, left, right = call(
        collect_kernel,
        [((3 * PACK, 128), bf16), own, own],
        [slots(3)],
        exchange(send),
    )
    left_all, right_all, send = call(
        triangle_kernel,
        [every_block, every_block, messages(3)],
        [slots(3), (3, SPAN, 128), (FOLD, 128)],
        lax.all_gather(gathered, "zhi", axis=0), left, right,
    )
    update, d_outpre, send = call(
        output_kernel,
        [tile, ((C, LANES), bf16), messages(2)],
        [
            padded, pltpu.VMEM((TI, TK, C), bf16), pltpu.SemaphoreType.DMA(()),
        ],
        exchange(send), projected, inside, vectors, grad, upstream, out_weights,
        written=(0,),
    )
    (send,) = call(
        back_kernel,
        [messages(2)],
        [slots(2), (2, SPAN, 128)],
        exchange(send), left_all, right_all,
    )
    (pair_grad,) = call(
        input_kernel,
        [tile],
        [padded],
        exchange(send), projected, inside, vectors, d_outpre, hat, inv_in, in_weights,
    )
    return update.transpose(1, 0, 2), pair_grad.transpose(1, 0, 2)


def solution(mesh):
    split = Mesh(mesh.devices.reshape(2, 4, 2, Q, 16 // Q, 2), ROWS + COLS)
    tiles = P(ROWS, COLS, None)
    in_specs = (tiles, P(), P(), P(), P(), P(), P(), P(), tiles)
    return jax.shard_map(
        body, mesh=split, in_specs=in_specs, out_specs=(tiles, tiles), check_vma=False
    )
```

```python
import jax
import jax.numpy as jnp
from jax import lax
from jax.experimental import pallas as pl
from jax.experimental.pallas import tpu as pltpu
from jax.sharding import Mesh, PartitionSpec as P

norm_eps = 1e-05
f32 = jnp.float32
bf16 = jnp.bfloat16
ROWS = ("xlo", "y", "core")
COLS = ("zhi", "zlo", "xhi")
OWNERS = ("zlo", "xhi", "xlo", "y", "core")
TK, TI, PAD = 24, 12, 16
LANES = TK * PAD
E, R, Q = 4, 16, 8
HELD = 8 // E
WIDTH = 128 // HELD
C = 128
N = 384
FOLD = N // 2
SPAN = N + 4 * 16
PACK = FOLD * TI // PAD
GROUP = FOLD - PACK
RF = R // 2


def dot(first_op, second_op, dims):
    return lax.dot_general(first_op, second_op, (dims, ((), ())), preferred_element_type=f32)


def swap_blocks(parts):
    parts = list(parts)
    block = lax.broadcasted_iota(jnp.int32, parts[0].shape, 1) // PAD
    for step in (4, 2, 1):
        upper = (block & step) != 0
        for a in range(8):
            if a & step:
                continue
            b = a | step
            low, high = parts[a], parts[b]
            if step == 4:
                turned = pltpu.roll(jnp.where(upper, low, high), 64, 1)
                parts[a] = jnp.where(upper, turned, low)
                parts[b] = jnp.where(upper, high, turned)
                continue
            parts[a] = jnp.where(upper, pltpu.roll(high, step * PAD, 1), low)
            parts[b] = jnp.where(upper, high, pltpu.roll(low, 128 - step * PAD, 1))
    return parts


def as_column(row):
    return jnp.broadcast_to(row, (C, C)).T[:, :1]


def padded_rows(tile, scratch):
    tile = tile.astype(f32)
    for i in range(PAD):
        part = tile[i] if i < TI else jnp.zeros((TK, C), f32)
        scratch[pl.ds(i, TK, stride=PAD), :] = part
    return scratch[...]


def unpadded_rows(values, scratch):
    scratch[...] = values
    return jnp.stack([scratch[pl.ds(i, TK, stride=PAD), :] for i in range(TI)]).astype(bf16)


def parts_of(slots):
    return [
        jnp.concatenate([slots[n, from_owner(held, e), :] for n in range(slots.shape[0])], axis=0)
        for held in range(HELD)
        for e in range(E)
    ]


def unpacked_rows(rows, kinds):
    slabs = [rows[n : n + R] for n in range(0, rows.shape[0], R)]
    return unpack_slabs(slabs, 3 * kinds)


def pack_rows(values):
    spare = lax.broadcasted_iota(jnp.int32, (PACK, 128), 1) % PAD >= TI
    last = values[PACK:]
    moved = [pltpu.roll(last, TI - (PAD - TI) * g, 1) for g in range(3)]
    return jnp.where(spare, jnp.concatenate(moved, axis=0), values[:PACK])


def unpack_rows(packed):
    lane = lax.broadcasted_iota(jnp.int32, (GROUP, 128), 1) % PAD
    last = jnp.zeros((GROUP, 128), f32)
    for g in range(3):
        back = pltpu.roll(packed[GROUP * g : GROUP * (g + 1)], 128 - TI + (PAD - TI) * g, 1)
        last = jnp.where(lane // (PAD - TI) == g, back, last)
    spare = lax.broadcasted_iota(jnp.int32, (PACK, 128), 1) % PAD >= TI
    return jnp.concatenate([jnp.where(spare, 0.0, packed), last], axis=0)


def own_block(shape):
    return lax.broadcasted_iota(jnp.int32, shape, 1) // WIDTH


def norm_rows(values):
    centered = values - jnp.mean(values, axis=1, keepdims=True)
    inv_std = lax.rsqrt(jnp.mean(centered * centered, axis=1, keepdims=True) + norm_eps)
    return centered * inv_std, inv_std


def slabs_of(values):
    return [values[:, 128 * t : 128 * (t + 1)] for t in range(3)]


def get_kind(slabs, kind):
    return jnp.concatenate(slabs[3 * kind : 3 * kind + 3], axis=1)


def pack_slabs(slabs):
    rest, packed = list(slabs), []
    lane = lax.broadcasted_iota(jnp.int32, rest[0].shape, 1) % PAD
    while len(rest) >= 4:
        for g in range(3):
            moved = pltpu.roll(rest[3], TI - (PAD - TI) * g, 1)
            packed.append(jnp.where(lane >= TI, moved, rest[g]))
        rest = rest[4:]
    return packed + rest


def unpack_slabs(packed, count):
    rest, slabs = list(packed), []
    lane = lax.broadcasted_iota(jnp.int32, rest[0].shape, 1) % PAD
    while count - len(slabs) >= 4:
        back = [pltpu.roll(rest[g], 128 - TI + (PAD - TI) * g, 1) for g in range(3)]
        last = jnp.where(lane < 4, back[0], jnp.where(lane < 8, back[1], back[2]))
        slabs += rest[:3] + [last]
        rest = rest[3:]
    return slabs + rest


def packed_count(kinds):
    return 3 * kinds - 3 * kinds // 4


def as_messages(packed):
    return jnp.concatenate(packed, axis=1).astype(bf16).reshape(C // HELD, HELD, -1)


def from_messages(received):
    rows = received[...].reshape(C, -1).astype(f32)
    return [rows[:, n : n + 128] for n in range(0, rows.shape[1], 128)]


def fill_slots(slots, received):
    for n, slab in enumerate(from_messages(received)):
        slots[n, :, :] = slab


def all_slots(slots):
    return [slots[n, :, :] for n in range(slots.shape[0])]


def from_owner(held, e):
    return pl.ds(HELD * R * e + held, R, stride=HELD)


def project_kernel(
    crop_hbm, pair_hbm, gain_hbm, bias_hbm, weights_hbm, out_gain_hbm, out_bias_hbm,
    cotangent_hbm, out_weights_hbm, send, projected, inside, vectors, grad, hat, inv_in, upstream,
    padded, crop, pair, gain, bias, weights, out_gain, out_bias,
    cotangent, out_weights, arrived,
):
    sources = (
        crop_hbm, pair_hbm, gain_hbm, bias_hbm, weights_hbm, out_gain_hbm, out_bias_hbm,
        cotangent_hbm, out_weights_hbm,
    )
    targets = (crop, pair, gain, bias, weights, out_gain, out_bias, cotangent, out_weights)
    loads = [
        pltpu.make_async_copy(source, target, arrived.at[n])
        for n, (source, target) in enumerate(zip(sources, targets))
    ]
    for load in loads:
        load.start()
    loads[1].wait()
    pair_hat, scale = norm_rows(padded_rows(pair[...], padded))
    hat[...] = pair_hat
    inv_in[...] = jnp.broadcast_to(scale, (LANES, C))
    loads[2].wait()
    loads[3].wait()
    normed = (pair_hat * gain[...] + bias[...]).astype(bf16)
    loads[4].wait()
    proj = dot(weights[...].T, normed, ((1,), (1,)))
    opened = jax.nn.sigmoid(proj[2 * C :])
    projected[: 2 * C] = proj[: 2 * C]
    projected[2 * C :] = opened

    loads[0].wait()
    row_pos = lax.axis_index(ROWS)
    col_pos = lax.axis_index(COLS)
    lane = lax.broadcasted_iota(jnp.int32, (8, LANES), 1)
    crop_rows = jnp.zeros((8, LANES), jnp.int32)
    crop_cols = jnp.full((8, LANES), -1, jnp.int32)
    for k in range(TK):
        crop_rows = jnp.where(lane // PAD == k, crop[row_pos * TK + k], crop_rows)
    for i in range(TI):
        crop_cols = jnp.where(lane % PAD == i, crop[col_pos * TI + i], crop_cols)
    same = (crop_rows == crop_cols).astype(f32)
    inside[...] = same
    mask = same[:1, :]
    left = mask * opened[:C] * proj[:C]
    right = mask * opened[C : 2 * C] * proj[C : 2 * C]
    for load in loads[5:]:
        load.wait()
    turned = padded_rows(cotangent[...], padded).T
    upstream[...] = turned
    d_value = (turned * opened[2 * C :]).astype(bf16)
    value_grad = dot(out_weights[...], d_value, ((1,), (0,))) * as_column(out_gain[...])
    grad[...] = value_grad
    masked_grad = jnp.where(mask > 0, value_grad, 0.0)
    send[...] = as_messages(
        pack_slabs(slabs_of(left) + slabs_of(right) + slabs_of(masked_grad))
    )
    vectors[...] = jnp.concatenate(
        [jnp.broadcast_to(v[...], (8, C)) for v in (gain, out_gain, out_bias)], axis=0
    )


def collect_kernel(received, gathered, left, right, slots):
    fill_slots(slots, received)
    parts = [unpacked_rows(part, 3) for part in swap_blocks(parts_of(slots))]
    for kind in range(3):
        pieces = []
        for t in range(3):
            for k in range(8):
                slab = parts[k][3 * kind + t]
                pieces.append(slab[:RF] + slab[RF:])
        whole = jnp.concatenate(pieces, axis=0)
        gathered[PACK * kind : PACK * (kind + 1)] = pack_rows(whole).astype(bf16)
        if kind < 2:
            (left, right)[kind][...] = whole.astype(bf16)


def residue_rows(column):
    return pl.ds(column % 2 * TI * R + column // 2, TI, stride=R)


def own_rows(block):
    lanes = own_block((WIDTH, 128))
    own = block[:WIDTH]
    for held in range(1, HELD):
        own = jnp.where(lanes == held, block[WIDTH * held : WIDTH * (held + 1)], own)
    return own


def unpack_own(rows):
    lane = lax.broadcasted_iota(jnp.int32, (6, 128), 1) % PAD
    back = [pltpu.roll(rows[6 * g : 6 * g + 6], 128 - TI + (PAD - TI) * g, 1) for g in range(3)]
    last = jnp.where(lane < 4, back[0], jnp.where(lane < 8, back[1], back[2]))
    return jnp.concatenate([rows[:18], last], axis=0)


def triangle_kernel(gathered, left, right, left_all, right_all, send, slots, ordered, folded):
    place = 2 * (lax.axis_index("zhi") % (Q // 2))
    spare = jnp.zeros((PAD - TI, 128), f32)
    for q in range(Q):
        lanes = slice(128 * q, 128 * (q + 1))
        left_all[:, lanes] = unpack_rows(gathered[q, :PACK].astype(f32)).astype(bf16)
        right_all[:, lanes] = unpack_rows(gathered[q, PACK : 2 * PACK].astype(f32)).astype(bf16)
    tri = dot(left_all[...], right[...], ((0,), (0,)))
    mirror = dot(right_all[...], left[...], ((0,), (0,)))
    for q in range(Q):
        folded[:PACK, :] = gathered[q, 2 * PACK :].astype(f32)
        own_i = [unpack_own(folded[pl.ds(place + half, TK, stride=RF), :]) for half in range(2)]
        pieces = []
        for e in range(E):
            pieces += [own_i[e // 2][e % 2 * TI : (e % 2 + 1) * TI], spare]
        blocks = (
            tri[128 * q : 128 * (q + 1)],
            mirror[128 * q : 128 * (q + 1)],
            jnp.concatenate(pieces * HELD, axis=0).T,
        )
        for kind, block in enumerate(blocks):
            own = own_rows(block)
            for e in range(E):
                ordered[kind, residue_rows(E * q + e), :] = own[PAD * e : PAD * e + TI]
    parts = swap_blocks(
        [
            jnp.concatenate(
                pack_slabs(
                    [
                        ordered[kind, (8 * t + i) * R : (8 * t + i + 1) * R]
                        for kind in range(3)
                        for t in range(3)
                    ]
                ),
                axis=0,
            )
            for i in range(8)
        ]
    )
    for held in range(HELD):
        for e in range(E):
            part = parts[held * E + e]
            for n in range(slots.shape[0]):
                slots[n, from_owner(held, e), :] = part[n * R : (n + 1) * R]
    send[...] = as_messages(all_slots(slots))


def norm_tri(slabs, kind, mask):
    tri = jnp.where(mask, get_kind(slabs, kind), 0.0)
    centered = tri - jnp.mean(tri, axis=0, keepdims=True)
    inv_out = lax.rsqrt(jnp.mean(centered * centered, axis=0, keepdims=True) + norm_eps)
    return centered * inv_out, inv_out


def norm_back(grad, tri_hat, inv_out, mask):
    first_mean = jnp.mean(grad, axis=0, keepdims=True)
    second_mean = jnp.mean(grad * tri_hat, axis=0, keepdims=True)
    return jnp.where(mask, inv_out * (grad - first_mean - tri_hat * second_mean), 0.0)


def output_kernel(
    received, projected, inside, vectors, grad, upstream, weights, update_hbm, d_outpre, send,
    padded, update, written,
):
    mask = inside[:1, :] > 0
    slabs = unpack_slabs(from_messages(received), 9)
    tri_hat, inv_out = norm_tri(slabs, 0, mask)
    normed_out = (tri_hat * as_column(vectors[8:9]) + as_column(vectors[16:17])).astype(bf16)
    gated_value = dot(weights[...].T, normed_out, ((1,), (0,)))
    gate = projected[4 * C :]
    update[...] = unpadded_rows((gate * gated_value).T, padded)
    write = pltpu.make_async_copy(update, update_hbm, written)
    write.start()
    d_tri = norm_back(grad[...], tri_hat, inv_out, mask)
    mirror_hat, mirror_inv = norm_tri(slabs, 1, mask)
    mirror_grad = jnp.where(mask, get_kind(slabs, 2), 0.0)
    d_mirror = norm_back(mirror_grad, mirror_hat, mirror_inv, mask)
    send[...] = as_messages(pack_slabs(slabs_of(d_tri) + slabs_of(d_mirror)))
    d_outpre[...] = (upstream[...] * gated_value * gate * (1.0 - gate)).astype(bf16)
    write.wait()


def padded_columns(rows):
    spare = jnp.zeros((PAD - TI, 128), f32)
    pieces = []
    for e in range(E):
        pieces += [rows[TI * e : TI * (e + 1)], spare]
    block = jnp.concatenate(pieces, axis=0)
    own = own_block((WIDTH, 128))
    return jnp.concatenate(
        [jnp.where(own == held, block, 0.0) for held in range(HELD)], axis=0
    ).astype(bf16)


def back_kernel(received, left_all, right_all, send, slots, ordered):
    fill_slots(slots, received)
    parts = [unpacked_rows(part, 2) for part in swap_blocks(parts_of(slots))]
    for kind in range(2):
        for t in range(3):
            for i in range(8):
                ordered[kind, pl.ds((8 * t + i) * R, R), :] = parts[i][3 * kind + t]
    by_i, by_j = (
        jnp.concatenate(
            [
                padded_columns(
                    jnp.concatenate([ordered[kind, residue_rows(E * q + e), :] for e in range(E)], axis=0)
                )
                for q in range(Q)
            ],
            axis=0,
        )
        for kind in range(2)
    )
    d_right = dot(left_all[...], by_i, ((1,), (0,)))
    d_left = dot(right_all[...], by_j, ((1,), (0,)))
    sides = (d_left, d_right)
    parts = swap_blocks(
        [
            jnp.concatenate(
                pack_slabs(
                    [
                        sides[side][(8 * t + k) * RF : (8 * t + k + 1) * RF]
                        for side in range(2)
                        for t in range(3)
                    ]
                ),
                axis=0,
            )
            for k in range(8)
        ]
    )
    for held in range(HELD):
        for e in range(E):
            part = parts[held * E + e]
            for n in range(slots.shape[0]):
                for half in range(2):
                    start = HELD * (R * e + RF * half) + held
                    slots[n, pl.ds(start, RF, stride=HELD), :] = part[n * RF : (n + 1) * RF]
    send[...] = as_messages(all_slots(slots))


def input_kernel(
    received, projected, inside, vectors, d_outpre, hat, inv_in, weights, pair_grad, padded
):
    slabs = unpack_slabs(from_messages(received), 6)
    mask = inside[:1, :]
    d_left = get_kind(slabs, 0) * mask
    d_right = get_kind(slabs, 1) * mask
    left_val, right_val = projected[:C], projected[C : 2 * C]
    left_sig, right_sig = projected[2 * C : 3 * C], projected[3 * C : 4 * C]
    d_proj = jnp.concatenate(
        [
            (d_left * left_sig).astype(bf16),
            (d_right * right_sig).astype(bf16),
            (d_left * left_val * left_sig * (1.0 - left_sig)).astype(bf16),
            (d_right * right_val * right_sig * (1.0 - right_sig)).astype(bf16),
            d_outpre[...],
        ],
        axis=0,
    )
    grad = dot(weights[...], d_proj, ((1,), (0,))).T * vectors[:1]
    first_mean = jnp.mean(grad, axis=1, keepdims=True)
    second_mean = jnp.mean(grad * hat[...], axis=1, keepdims=True)
    pair_grad[...] = unpadded_rows(
        inv_in[...] * (grad - first_mean - hat[...] * second_mean), padded
    )


def call(kernel, outs, scratch, *operands, inputs=None, written=()):
    inputs = inputs or [pltpu.VMEM] * len(operands)
    return pl.pallas_call(
        kernel,
        out_shape=[jax.ShapeDtypeStruct(shape, dtype) for shape, dtype in outs],
        in_specs=[pl.BlockSpec(memory_space=space) for space in inputs],
        out_specs=[
            pl.BlockSpec(memory_space=pl.ANY if n in written else pltpu.VMEM)
            for n in range(len(outs))
        ],
        scratch_shapes=[
            pltpu.VMEM(shape, f32) if isinstance(shape, tuple) else shape for shape in scratch
        ],
        compiler_params=pltpu.CompilerParams(vmem_limit_bytes=40 * 1024 * 1024),
        name=kernel.__name__,
    )(*operands)


def exchange(messages):
    return lax.all_to_all(messages, OWNERS, 0, 0, tiled=True)


def body(pair, crop, in_gain, in_bias, in_weights, out_gain, out_bias, out_weights, cotangent):
    padded = (LANES, C)
    tile = ((TI, TK, C), bf16)
    pair = pair.transpose(1, 0, 2)
    cotangent = cotangent.transpose(1, 0, 2)
    in_gain, in_bias, out_gain, out_bias = (
        v.reshape(1, C) for v in (in_gain, in_bias, out_gain, out_bias)
    )
    def messages(kinds):
        return ((C // HELD, HELD, 128 * packed_count(kinds)), bf16)

    def slots(kinds):
        return (packed_count(kinds), C, 128)

    every_block = ((FOLD, Q * 128), bf16)
    own = ((FOLD, 128), bf16)
    send, projected, inside, vectors, grad, hat, inv_in, upstream = call(
        project_kernel,
        [
            messages(3), ((5 * C, LANES), f32), ((8, LANES), f32), ((24, C), f32), ((C, LANES), f32),
            (padded, f32), (padded, f32), ((C, LANES), f32),
        ],
        [
            padded, pltpu.SMEM((N,), jnp.int32),
            pltpu.VMEM((TI, TK, C), bf16), (1, C), (1, C), pltpu.VMEM((C, 5 * C), bf16),
            (1, C), (1, C), pltpu.VMEM((TI, TK, C), bf16), pltpu.VMEM((C, C), bf16),
            pltpu.SemaphoreType.DMA((9,)),
        ],
        *(
            pltpu.with_memory_space_constraint(v, pltpu.HBM)
            for v in (
                crop, pair, in_gain, in_bias, in_weights, out_gain, out_bias, cotangent, out_weights
            )
        ),
        inputs=[pl.ANY] * 9,
    )
    gathered, left, right = call(
        collect_kernel,
        [((3 * PACK, 128), bf16), own, own],
        [slots(3)],
        exchange(send),
    )
    left_all, right_all, send = call(
        triangle_kernel,
        [every_block, every_block, messages(3)],
        [slots(3), (3, SPAN, 128), (FOLD, 128)],
        lax.all_gather(gathered, "zhi", axis=0), left, right,
    )
    update, d_outpre, send = call(
        output_kernel,
        [tile, ((C, LANES), bf16), messages(2)],
        [
            padded, pltpu.VMEM((TI, TK, C), bf16), pltpu.SemaphoreType.DMA(()),
        ],
        exchange(send), projected, inside, vectors, grad, upstream, out_weights,
        written=(0,),
    )
    (send,) = call(
        back_kernel,
        [messages(2)],
        [slots(2), (2, SPAN, 128)],
        exchange(send), left_all, right_all,
    )
    (pair_grad,) = call(
        input_kernel,
        [tile],
        [padded],
        exchange(send), projected, inside, vectors, d_outpre, hat, inv_in, in_weights,
    )
    return update.transpose(1, 0, 2), pair_grad.transpose(1, 0, 2)


def solution(mesh):
    split = Mesh(mesh.devices.reshape(2, 4, 2, Q, 16 // Q, 2), ROWS + COLS)
    tiles = P(ROWS, COLS, None)
    in_specs = (tiles, P(), P(), P(), P(), P(), P(), P(), tiles)
    return jax.shard_map(
        body, mesh=split, in_specs=in_specs, out_specs=(tiles, tiles), check_vma=False
    )
```
